32 devices in a mesh: seq: 8 (over z, y), head: 4 (over x, core).
Axes of the slice: x: 2, y: 2, z: 4, core: 2. Of those that a mesh axis runs over, the one named last changes fastest.
Arguments:
- tokens: bfloat16 [2048, 2048], P('seq')
- w_qkv: bfloat16 [2048, 3, 2048], P(None, None, 'head'), may hold values from -0.125 to 0.125
- w_out: bfloat16 [2048, 2048], P('head'), may hold values from -0.125 to 0.125
- norm_gain: float32 [2048], replicated, may hold values from 0.25 to 1.75
- w_label: bfloat16 [2048, 128], replicated, may hold values from -0.125 to 0.125
- offset_mid: int32 [16], P('head'), may hold values from 0 to 7
- offset_far: int32 [16], P('head'), may hold values from 0 to 7
Outputs:
- logits: float32 [2048, 128], P('seq')
The draws below stay inside these ranges and needn't reach their ends.
All inputs are finite; a program needn't handle non-finite values.
Results may differ from the reference program's by a relative error of at most 0.023.
The reference program's roundings to bfloat16 on the way (of `qkv`, `attn` and `scaled`) count: a program that leaves them out, or rounds other values in their place, can miss the bound.
Values may be sent and summed in bfloat16 or wider, within the bound.
A program may use at most 64 MiB of HBM per device.

```python
import jax
import jax.numpy as jnp
from jax import lax

D = 2048
HEADS = 16
HEAD_DIM = 128
CLASSES = 128
SPAN = 8
TOK_DEV = 256
TOKENS = 2048
N_SEQ = 8
N_HEAD = 4


def draw_tokens(key, part):
    base = jax.random.normal(jax.random.fold_in(key, 11), (TOKENS, D), jnp.float32)
    base = jnp.clip(base, -6.0, 6.0) * 4.0
    return base.astype(jnp.bfloat16)


def place_ends(values, key, least, largest):
    longest = values.shape.index(max(values.shape))
    spots = []
    for shift in (0, 1):
        where = [jax.random.randint(jax.random.fold_in(key, axis), (), 0, length) for axis, length in enumerate(values.shape)]
        where[longest] = (where[longest] + shift) % values.shape[longest]
        spots.append(tuple(where))
    return values.at[spots[0]].set(least).at[spots[1]].set(largest)


def block_levels(own_key, shape, shards, least, top_value):
    def one(dim, shards_of):
        draws = jax.random.uniform(jax.random.fold_in(jax.random.fold_in(own_key, 6), dim), (shards_of,), jnp.float32, least / len(shards), top_value / len(shards))
        return jnp.repeat(jnp.exp(draws), shape[dim] // shards_of).reshape((-1,) + (1,) * (len(shape) - dim - 1))

    loudness = one(*shards[0])
    for cut in shards[1:]:
        loudness = loudness * one(*cut)
    return loudness


def scatter_about(key, shape, scale, bound, split=(), kind=jnp.bfloat16):
    result = jax.random.normal(key, shape, jnp.float32) * scale
    if len(split) > 0:
        result = block_levels(key, shape, split, -0.22, 0.18) * result
    return jnp.clip(result, min=-bound, max=bound).astype(kind)


def setup_inputs(seed: int = 0) -> dict:
    key_of = jax.random.split(jax.random.key(seed), 8)
    tokens = draw_tokens(jax.random.fold_in(key_of[7], 71), 0)
    w_qkv = scatter_about(key_of[1], (D, 3, D), D ** -0.5, 0.125, ((2, 4),))
    w_out = scatter_about(key_of[2], (D, D), D ** -0.5, 0.125, ((0, 4),))
    norm_gain = jnp.clip(1.0 + 0.15 * jax.random.normal(key_of[3], (D,), jnp.float32), 0.25, 1.75)
    w_label = scatter_about(key_of[4], (D, CLASSES), D ** -0.5, 0.125)
    offset_mid = place_ends(jax.random.randint(key_of[5], (HEADS,), 0, SPAN), jax.random.fold_in(key_of[5], 1), 0, SPAN - 1).astype(jnp.int32)
    offset_far = place_ends(jax.random.randint(key_of[6], (HEADS,), 0, N_SEQ), jax.random.fold_in(key_of[6], 1), 0, N_SEQ - 1).astype(jnp.int32)
    return {"tokens": tokens, "w_qkv": w_qkv, "w_out": w_out, "norm_gain": norm_gain, "w_label": w_label, "offset_mid": offset_mid, "offset_far": offset_far}


def attend(queries, keys, values):
    scores = jnp.einsum('rhe,she->hrs', queries.astype(jnp.float32), keys.astype(jnp.float32)) / jnp.sqrt(jnp.float32(HEAD_DIM))
    top = lax.optimization_barrier(jnp.max(scores, axis=-1))
    weights = jnp.exp(scores - top[..., None])
    total = lax.optimization_barrier(jnp.sum(weights, axis=-1))
    weights = weights.astype(jnp.bfloat16).astype(jnp.float32)
    summed = jnp.einsum('hrs,she->rhe', weights, values.astype(jnp.float32))
    return (top.T, total.T, summed)

def select_rows(array, offsets, rate):
    rows = array.shape[0] // rate
    shaped = array.reshape(rows, rate, array.shape[1], array.shape[2])
    index = jnp.broadcast_to(offsets.astype(jnp.int32)[None, None, :, None], (rows, 1, array.shape[1], array.shape[2]))
    return jnp.take_along_axis(shaped, index, axis=1)[:, 0]

def spread_rows(parts, offsets, rate):
    top, total, summed = parts
    rows = top.shape[0]
    marks = jnp.arange(rate, dtype=jnp.int32)[None, :, None] == offsets.astype(jnp.int32)[None, None, :]
    top_full = jnp.where(marks, top[:, None, :], jnp.float32(-1e+30)).reshape(rows * rate, -1)
    total_full = jnp.where(marks, total[:, None, :], jnp.float32(0.0)).reshape(rows * rate, -1)
    sum_full = jnp.where(marks[..., None], summed[:, None], jnp.float32(0.0)).reshape(rows * rate, summed.shape[1], summed.shape[2])
    return (top_full, total_full, sum_full)

def branch(queries, keys, values, offsets, rate, segment, turn):
    sel_q = select_rows(queries, offsets, rate)
    sel_k = select_rows(keys, offsets, rate)
    sel_v = select_rows(values, offsets, rate)
    if turn:
        sel_q = jnp.roll(sel_q, turn, axis=0)
        sel_k = jnp.roll(sel_k, turn, axis=0)
        sel_v = jnp.roll(sel_v, turn, axis=0)
    groups = sel_q.shape[0] // segment
    shaped = lambda a: a.reshape(groups, segment, a.shape[1], a.shape[2])
    top, total, summed = lax.map(lambda t: attend(t[0], t[1], t[2]), (shaped(sel_q), shaped(sel_k), shaped(sel_v)))
    top = top.reshape(-1, HEADS)
    total = total.reshape(-1, HEADS)
    summed = summed.reshape(-1, HEADS, HEAD_DIM)
    if turn:
        top = jnp.roll(top, -turn, axis=0)
        total = jnp.roll(total, -turn, axis=0)
        summed = jnp.roll(summed, -turn, axis=0)
    return spread_rows((top, total, summed), offsets, rate)

def reference(tokens, w_qkv, w_out, norm_gain, w_label, offset_mid, offset_far):
    qkv = jnp.dot(tokens, w_qkv.reshape(D, 3 * D), preferred_element_type=jnp.float32).astype(jnp.bfloat16)
    qkv = qkv.reshape(TOKENS, 3, HEADS, HEAD_DIM)
    queries, keys, values = (qkv[:, 0], qkv[:, 1], qkv[:, 2])
    zeros = jnp.zeros((HEADS,), jnp.int32)
    middle_turn = SPAN // 2 * (TOK_DEV // SPAN)
    branches = [branch(queries, keys, values, zeros, 1, TOK_DEV, 0), branch(queries, keys, values, offset_mid, SPAN, TOK_DEV, middle_turn), branch(queries, keys, values, offset_far, N_SEQ, TOK_DEV, 0)]
    peak = jnp.maximum(jnp.maximum(branches[0][0], branches[1][0]), branches[2][0])
    upper = jnp.zeros((TOKENS, HEADS, HEAD_DIM), jnp.float32)
    lower = jnp.zeros((TOKENS, HEADS), jnp.float32)
    for top, total, summed in branches:
        factor = jnp.exp(top - peak)
        upper = upper + factor[..., None] * summed
        lower = lower + factor * total
    attn = (upper / lower[..., None]).astype(jnp.bfloat16).reshape(TOKENS, D)
    group = D // N_HEAD
    mixed = tokens.astype(jnp.float32)
    for index in range(N_HEAD):
        part = jnp.dot(attn[:, index * group:(index + 1) * group], w_out[index * group:(index + 1) * group], preferred_element_type=jnp.float32)
        mixed = mixed + part.astype(jnp.bfloat16).astype(jnp.float32)
    mean_sq = lax.optimization_barrier(jnp.mean(mixed * mixed, axis=-1))
    scaled = (mixed * norm_gain).astype(jnp.bfloat16)
    product = jnp.dot(scaled, w_label, preferred_element_type=jnp.float32)
    return product / jnp.sqrt(mean_sq + 1e-05)[:, None]
```

```python
import functools

import jax
import jax.numpy as jnp
from jax import lax
from jax.experimental import pallas as pl
from jax.experimental.pallas import tpu as pltpu
from jax.sharding import PartitionSpec as P

MESH = pl.DeviceIdType.MESH

SPAN = 8


def from_behind(block, axis, distance):
    devices = range(lax.axis_size(axis))
    route = [((i - distance) % len(devices), i) for i in devices]
    return lax.ppermute(block, axis, route)


def attend(queries, keys, values):
    scores = jnp.einsum(
        "rhe,she->hrs", queries, keys, preferred_element_type=jnp.float32
    ) / jnp.sqrt(jnp.float32(queries.shape[2]))
    top = jnp.max(scores, axis=-1)
    weights = jnp.exp(scores - top[..., None])
    total = jnp.sum(weights, axis=-1)
    summed = jnp.einsum(
        "hrs,she->rhe", weights.astype(jnp.bfloat16), values, preferred_element_type=jnp.float32
    )
    return (top.T, total.T, summed)


def select_rows(array, offsets, rate):
    rows = array.shape[0] // rate
    shaped = array.reshape(rows, rate, array.shape[1], array.shape[2])
    marks = jnp.arange(rate, dtype=jnp.int32)[None, :, None] == offsets[None, None, :]
    return jnp.sum(jnp.where(marks[..., None], shaped, jnp.zeros_like(shaped)), axis=1)


def spread_rows(parts, offsets, rate):
    top, total, summed = parts
    rows = top.shape[0]
    marks = jnp.arange(rate, dtype=jnp.int32)[None, :, None] == offsets[None, None, :]
    top_full = jnp.where(marks, top[:, None, :], jnp.float32(-1e30)).reshape(rows * rate, -1)
    total_full = jnp.where(marks, total[:, None, :], jnp.float32(0.0)).reshape(rows * rate, -1)
    sum_full = jnp.where(marks[..., None], summed[:, None], jnp.float32(0.0)).reshape(
        rows * rate, summed.shape[1], summed.shape[2]
    )
    return (top_full, total_full, sum_full)


def body(tokens, w_qkv, w_out, norm_gain, w_label, offset_mid, offset_far):
    tok_rows = tokens.shape[0]
    local_heads = offset_mid.shape[0]
    head_size = w_qkv.shape[2] // local_heads
    qkv = jnp.einsum("td,dce->tce", tokens, w_qkv, preferred_element_type=jnp.float32).astype(
        jnp.bfloat16
    )
    qkv = qkv.reshape(tok_rows, 3, local_heads, head_size)
    queries, keys, values = (qkv[:, 0], qkv[:, 1], qkv[:, 2])
    seq_count = lax.axis_size("seq")
    near = attend(queries, keys, values)
    mid_q = select_rows(queries, offset_mid, SPAN)
    mid_kv = jnp.stack(
        [select_rows(keys, offset_mid, SPAN), select_rows(values, offset_mid, SPAN)], axis=0
    )
    mid_rows = mid_kv.shape[1]
    position = (lax.axis_index("seq") + SPAN // 2) % SPAN
    lower_pieces = []
    upper_pieces = []
    for step_back in range(1, SPAN):
        lower_pieces.insert(0, from_behind(mid_kv, "seq", step_back))
        upper_pieces.append(from_behind(mid_kv, "seq", -step_back))
    window = jnp.concatenate(lower_pieces + [mid_kv] + upper_pieces, axis=1)
    gathered = lax.dynamic_slice_in_dim(
        window, (SPAN - 1 - position) * mid_rows, SPAN * mid_rows, 1
    )
    middle = spread_rows(attend(mid_q, gathered[0], gathered[1]), offset_mid, SPAN)
    far_q = select_rows(queries, offset_far, seq_count)
    far_kv = jnp.stack(
        [select_rows(keys, offset_far, seq_count), select_rows(values, offset_far, seq_count)],
        axis=0,
    )
    far_all = lax.all_gather(far_kv, "seq", axis=1, tiled=True)
    distant = spread_rows(attend(far_q, far_all[0], far_all[1]), offset_far, seq_count)
    branches = [near, middle, distant]
    peak = jnp.maximum(jnp.maximum(near[0], middle[0]), distant[0])
    upper = jnp.zeros((tok_rows, local_heads, head_size), jnp.float32)
    lower = jnp.zeros((tok_rows, local_heads), jnp.float32)
    for top, total, summed in branches:
        factor = jnp.exp(top - peak)
        upper = upper + factor[..., None] * summed
        lower = lower + factor * total
    attn = (
        (upper / lower[..., None]).astype(jnp.bfloat16).reshape(tok_rows, local_heads * head_size)
    )
    partial_out = jnp.dot(attn, w_out, preferred_element_type=jnp.float32)
    projected = lax.psum(partial_out.astype(jnp.bfloat16), "head").astype(jnp.float32)
    mixed = tokens.astype(jnp.float32) + projected
    mean_sq = jnp.mean(mixed * mixed, axis=-1)
    scaled = (mixed * norm_gain).astype(jnp.bfloat16)
    product = jnp.dot(scaled, w_label, preferred_element_type=jnp.float32)
    return product / jnp.sqrt(mean_sq + 1e-05)[:, None]


def softmax_parts(queries, keys, values):
    scale = 1.0 / queries.shape[1] ** 0.5
    scores = (
        lax.dot_general(
            queries, keys, (((1,), (1,)), ((), ())), preferred_element_type=jnp.float32
        )
        * scale
    )
    top = jnp.max(scores, axis=-1, keepdims=True)
    weights = jnp.exp(scores - top)
    total = jnp.sum(weights, axis=-1, keepdims=True)
    summed = jnp.dot(weights.astype(jnp.bfloat16), values, preferred_element_type=jnp.float32)
    return summed / total, top + jnp.log(total)


def kernel(
    tok_hbm, wqkv_hbm, wout_hbm, gain_hbm, wlabel_hbm, off_mid, off_far, out_ref,
    tok, wqkv, wout, gain, wlabel, qkv, pair_out, pair_in, ret_o, ret_l, got_o, got_l,
    attn, parts, sib_in, x_out, x_in, log_out, log_in,
    load_sem, w_sem, a2a_send, a2a_recv, o_send, o_recv, l_send, l_recv,
    sib_send, sib_recv, x_send, x_recv, log_send, log_recv,
):
    seq = lax.axis_index("seq")
    head = lax.axis_index("head")
    n_seq = pair_in.shape[0]
    n_head = log_in.shape[0]
    rows = tok.shape[0]
    picked = pair_in.shape[1]
    hd = got_o.shape[2]
    heads = n_seq // 2
    core = lax.rem(head, 2)
    chip = head // 2
    sibling = head + 1 - 2 * core
    across = lax.rem(head + 2, n_head)

    barrier = pltpu.get_barrier_semaphore()
    for d in range(1, n_seq):
        pl.semaphore_signal(
            barrier, inc=1, device_id=(lax.rem(seq + d, n_seq), head), device_id_type=MESH
        )
    for d in range(1, n_head):
        pl.semaphore_signal(
            barrier, inc=1, device_id=(seq, lax.rem(head + d, n_head)), device_id_type=MESH
        )

    wide = wqkv.shape[2]
    halves = qkv.shape[2] // wide
    loads = [pltpu.make_async_copy(tok_hbm, tok, load_sem.at[0])]
    w_loads = []
    for half in range(halves):
        for c in range(3):
            k = half * 3 + c
            w_loads.append(
                pltpu.make_async_copy(
                    wqkv_hbm.at[c, :, pl.ds(half * wide, wide)], wqkv.at[k], w_sem.at[k]
                )
            )
    loads.append(pltpu.make_async_copy(wout_hbm, wout, load_sem.at[1]))
    loads.append(pltpu.make_async_copy(gain_hbm, gain, load_sem.at[2]))
    loads.append(pltpu.make_async_copy(wlabel_hbm, wlabel, load_sem.at[3]))
    loads[0].start()
    for load in w_loads:
        load.start()
    for load in loads[1:]:
        load.start()

    def pair_copy(j):
        return pltpu.make_async_remote_copy(
            src_ref=pair_out.at[j], dst_ref=pair_in.at[seq],
            send_sem=a2a_send.at[j], recv_sem=a2a_recv.at[seq],
            device_id=(j, head), device_id_type=MESH,
        )

    def pair_arrival(i):
        return pltpu.make_async_remote_copy(
            src_ref=pair_out.at[i], dst_ref=pair_in.at[i],
            send_sem=a2a_send.at[i], recv_sem=a2a_recv.at[i],
            device_id=(i, head), device_id_type=MESH,
        )

    sel_row = lax.broadcasted_iota(jnp.int32, (picked, rows), 0)
    sel_tok = lax.broadcasted_iota(jnp.int32, (picked, rows), 1)
    loads[0].wait()
    for half in range(halves):
        for c in range(3):
            k = half * 3 + c
            w_loads[k].wait()
            qkv[c, :, half * wide : (half + 1) * wide] = jnp.dot(
                tok[...], wqkv[k], preferred_element_type=jnp.float32
            ).astype(jnp.bfloat16)
        if half == 0:
            pl.semaphore_wait(barrier, n_seq + n_head - 2)
        for h in range(half * wide // hd, (half + 1) * wide // hd):
            cols = slice(h * hd, (h + 1) * hd)
            mine = jnp.concatenate([qkv[c, :, cols] for c in range(3)], axis=1)
            for b, off in enumerate((off_mid, off_far)):
                j = b * heads + h
                one_hot = (sel_tok == sel_row * SPAN + off[h]).astype(jnp.bfloat16)
                pair_out[j] = jnp.dot(
                    one_hot, mine, preferred_element_type=jnp.float32
                ).astype(jnp.bfloat16)

                @pl.when(seq != j)
                def _(j=j):
                    pair_copy(j).start()

    pair_in[seq] = pair_out[seq]

    near = []
    for h in range(heads):
        cols = slice(h * hd, (h + 1) * hd)
        near.append(softmax_parts(qkv[0, :, cols], qkv[1, :, cols], qkv[2, :, cols]))

    for i in range(n_seq):

        @pl.when(seq != i)
        def _(i=i):
            pair_arrival(i).wait_recv()

    everyone = n_seq * picked
    pq, pk, pv = (
        pair_in[:, :, c * hd : (c + 1) * hd].reshape(everyone, hd) for c in range(3)
    )
    o, lse = softmax_parts(pq, pk, pv)
    ret_o[...] = o.astype(jnp.bfloat16).reshape(n_seq, picked, hd)
    r0 = lax.broadcasted_iota(jnp.int32, (everyone, everyone), 0)
    r1 = lax.broadcasted_iota(jnp.int32, (everyone, everyone), 1)
    lse_row = jnp.sum(jnp.where(r0 == r1, lse, 0.0), axis=0, keepdims=True)
    per_tile = hd // picked
    for t in range(everyone // hd):
        ret_l[t] = jnp.broadcast_to(lse_row[:, t * hd : (t + 1) * hd], ret_l.shape[1:])

    def back_copies(i, slot):
        return (
            pltpu.make_async_remote_copy(
                src_ref=ret_o.at[i], dst_ref=got_o.at[slot],
                send_sem=o_send.at[i], recv_sem=o_recv.at[slot],
                device_id=(i, head), device_id_type=MESH,
            ),
            pltpu.make_async_remote_copy(
                src_ref=ret_l.at[i // per_tile], dst_ref=got_l.at[slot],
                send_sem=l_send.at[i], recv_sem=l_recv.at[slot],
                device_id=(i, head), device_id_type=MESH,
            ),
        )

    for i in range(n_seq):

        @pl.when(seq != i)
        def _(i=i):
            for copy in back_copies(i, seq):
                copy.start()

    got_o[seq] = ret_o[seq]
    got_l[seq] = ret_l[seq // per_tile]

    tok_col = lax.broadcasted_iota(jnp.int32, (rows, hd), 0)
    lane = lax.broadcasted_iota(jnp.int32, (rows, hd), 1)
    base = lax.rem(seq, per_tile) * picked
    tok_sel = lax.broadcasted_iota(jnp.int32, (rows, picked), 0)
    row_sel = lax.broadcasted_iota(jnp.int32, (rows, picked), 1)
    tok_one = lax.broadcasted_iota(jnp.int32, (rows, 1), 0)
    for h in range(heads):
        terms = [near[h]]
        marks = [None]
        for b, off in enumerate((off_mid, off_far)):
            j = b * heads + h

            @pl.when(seq != j)
            def _(j=j):
                for copy in back_copies(j, j):
                    copy.wait_recv()

            spot = off[h]
            hit = (lane - base) * SPAN + spot == tok_col
            lse_col = jnp.sum(
                jnp.where(hit, got_l[j, 0:1, :], 0.0), axis=-1, keepdims=True
            )
            one_hot = (tok_sel == row_sel * SPAN + spot).astype(jnp.bfloat16)
            spread = jnp.dot(one_hot, got_o[j], preferred_element_type=jnp.float32)
            mark = lax.rem(tok_one, SPAN) == spot
            terms.append((spread, jnp.where(mark, lse_col, -1e30)))
            marks.append(mark)
        peak = jnp.maximum(jnp.maximum(terms[0][1], terms[1][1]), terms[2][1])
        upper = jnp.zeros((rows, hd), jnp.float32)
        lower = jnp.zeros((rows, 1), jnp.float32)
        for (o, lse), mark in zip(terms, marks):
            factor = jnp.exp(lse - peak)
            if mark is not None:
                factor = jnp.where(mark, factor, 0.0)
            upper = upper + factor * o
            lower = lower + factor
        attn[:, h * hd : (h + 1) * hd] = (upper / lower).astype(jnp.bfloat16)

    chunks = x_in.shape[0]
    part = x_in.shape[1]
    width = x_in.shape[2]

    def sib_copy(s, n):
        return pltpu.make_async_remote_copy(
            src_ref=parts.at[s, n, 1 - core], dst_ref=sib_in.at[s, n],
            send_sem=sib_send.at[s, n], recv_sem=sib_recv.at[s, n],
            device_id=(seq, sibling), device_id_type=MESH,
        )

    def x_copy(n):
        return pltpu.make_async_remote_copy(
            src_ref=x_out.at[n], dst_ref=x_in.at[n],
            send_sem=x_send.at[n], recv_sem=x_recv.at[n],
            device_id=(seq, across), device_id_type=MESH,
        )

    for load in loads[1:]:
        load.wait()
    for s in range(2):
        place = (1 - chip) if s == 0 else chip
        left = attn[pl.ds(pl.multiple_of(place * 2 * part, 2 * part), 2 * part), :]
        for n in range(chunks):
            parts[s, n] = (
                jnp.dot(
                    left, wout[:, n * width : (n + 1) * width],
                    preferred_element_type=jnp.float32,
                )
                .astype(jnp.bfloat16)
                .reshape(2, part, width)
            )
            sib_copy(s, n).start()
        if s == 0:
            for n in range(chunks):
                sib_copy(0, n).wait_recv()
                x_out[n] = (
                    parts[0, n, core].astype(jnp.float32) + sib_in[0, n].astype(jnp.float32)
                ).astype(jnp.bfloat16)
                x_copy(n).start()

    squares = jnp.zeros((part, 1), jnp.float32)
    product = jnp.zeros((part, wlabel.shape[1]), jnp.float32)
    here = pl.ds(pl.multiple_of(head * part, part), part)
    for n in range(chunks):
        cols = slice(n * width, (n + 1) * width)
        sib_copy(1, n).wait_recv()
        x_copy(n).wait_recv()
        summed = parts[1, n, core].astype(jnp.float32) + sib_in[1, n].astype(jnp.float32)
        mixed = tok[here, cols].astype(jnp.float32) + (summed + x_in[n].astype(jnp.float32))
        squares = squares + jnp.sum(mixed * mixed, axis=-1, keepdims=True)
        scaled = (mixed * gain[:, cols]).astype(jnp.bfloat16)
        product = product + jnp.dot(scaled, wlabel[cols, :], preferred_element_type=jnp.float32)
    log_out[...] = product / jnp.sqrt(squares / tok.shape[1] + 1e-05)

    def log_copy(p, slot):
        return pltpu.make_async_remote_copy(
            src_ref=log_out, dst_ref=log_in.at[slot],
            send_sem=log_send.at[p], recv_sem=log_recv.at[slot],
            device_id=(seq, p), device_id_type=MESH,
        )

    for p in range(n_head):

        @pl.when(head != p)
        def _(p=p):
            log_copy(p, head).start()

    log_in[head] = log_out[...]
    for p in range(n_head):

        @pl.when(head != p)
        def _(p=p):
            log_copy(p, p).wait_recv()

        out_ref[p * part : (p + 1) * part, :] = log_in[p]

    for j in range(n_seq):

        @pl.when(seq != j)
        def _(j=j):
            pair_copy(j).wait_send()
            for copy in back_copies(j, seq):
                copy.wait_send()

    for n in range(chunks):
        sib_copy(0, n).wait_send()
        sib_copy(1, n).wait_send()
        x_copy(n).wait_send()
    for p in range(n_head):

        @pl.when(head != p)
        def _(p=p):
            log_copy(p, head).wait_send()


def fused_body(n_seq, n_head, tokens, w_qkv, w_out, norm_gain, w_label, offset_mid, offset_far):
    rows, width = tokens.shape
    heads = offset_mid.shape[0]
    own = w_qkv.shape[2]
    hd = own // heads
    classes = w_label.shape[1]
    picked = rows // SPAN
    part = rows // n_head
    chunks = 4
    span = width // chunks
    bf16, f32 = jnp.bfloat16, jnp.float32
    dma = pltpu.SemaphoreType.DMA
    anywhere = pl.BlockSpec(memory_space=pl.ANY)
    scalars = pl.BlockSpec(memory_space=pltpu.SMEM)
    return pl.pallas_call(
        kernel,
        out_shape=jax.ShapeDtypeStruct((rows, classes), f32),
        in_specs=[anywhere] * 5 + [scalars] * 2,
        out_specs=pl.BlockSpec(memory_space=pltpu.VMEM),
        scratch_shapes=[
            pltpu.VMEM((rows, width), bf16),
            pltpu.VMEM((6, width, own // 2), bf16),
            pltpu.VMEM((own, width), bf16),
            pltpu.VMEM((1, width), f32),
            pltpu.VMEM((width, classes), bf16),
            pltpu.VMEM((3, rows, own), bf16),
            pltpu.VMEM((n_seq, picked, 3 * hd), bf16),
            pltpu.VMEM((n_seq, picked, 3 * hd), bf16),
            pltpu.VMEM((n_seq, picked, hd), bf16),
            pltpu.VMEM((n_seq * picked // hd, 8, hd), f32),
            pltpu.VMEM((n_seq, picked, hd), bf16),
            pltpu.VMEM((n_seq, 8, hd), f32),
            pltpu.VMEM((rows, own), bf16),
            pltpu.VMEM((2, chunks, 2, part, span), bf16),
            pltpu.VMEM((2, chunks, part, span), bf16),
            pltpu.VMEM((chunks, part, span), bf16),
            pltpu.VMEM((chunks, part, span), bf16),
            pltpu.VMEM((part, classes), f32),
            pltpu.VMEM((n_head, part, classes), f32),
            dma((4,)), dma((6,)), dma((n_seq,)), dma((n_seq,)),
            dma((n_seq,)), dma((n_seq,)), dma((n_seq,)), dma((n_seq,)),
            dma((2, chunks)), dma((2, chunks)), dma((chunks,)), dma((chunks,)),
            dma((n_head,)), dma((n_head,)),
        ],
        compiler_params=pltpu.CompilerParams(
            collective_id=0, has_side_effects=True, vmem_limit_bytes=56 * 2**20
        ),
    )(
        tokens, jnp.transpose(w_qkv, (1, 0, 2)), w_out, norm_gain[None, :], w_label,
        offset_mid, offset_far,
    )


def solution(mesh):
    n_seq, n_head = mesh.shape["seq"], mesh.shape["head"]
    run = body
    if n_seq == SPAN and n_head == 4:
        run = functools.partial(fused_body, n_seq, n_head)
    return jax.shard_map(
        run,
        mesh=mesh,
        in_specs=(
            P("seq", None),
            P(None, None, "head"),
            P("head", None),
            P(),
            P(),
            P("head"),
            P("head"),
        ),
        out_specs=P("seq", None),
        check_vma=False,
    )
```

```python
import functools

import jax
import jax.numpy as jnp
from jax import lax
from jax.experimental import pallas as pl
from jax.experimental.pallas import tpu as pltpu
from jax.sharding import PartitionSpec as P

MESH = pl.DeviceIdType.MESH

SPAN = 8


def from_behind(block, axis, distance):
    devices = range(lax.axis_size(axis))
    route = [((i - distance) % len(devices), i) for i in devices]
    return lax.ppermute(block, axis, route)


def attend(queries, keys, values):
    scores = jnp.einsum(
        "rhe,she->hrs", queries, keys, preferred_element_type=jnp.float32
    ) / jnp.sqrt(jnp.float32(queries.shape[2]))
    top = jnp.max(scores, axis=-1)
    weights = jnp.exp(scores - top[..., None])
    total = jnp.sum(weights, axis=-1)
    summed = jnp.einsum(
        "hrs,she->rhe", weights.astype(jnp.bfloat16), values, preferred_element_type=jnp.float32
    )
    return (top.T, total.T, summed)


def select_rows(array, offsets, rate):
    rows = array.shape[0] // rate
    shaped = array.reshape(rows, rate, array.shape[1], array.shape[2])
    marks = jnp.arange(rate, dtype=jnp.int32)[None, :, None] == offsets[None, None, :]
    return jnp.sum(jnp.where(marks[..., None], shaped, jnp.zeros_like(shaped)), axis=1)


def spread_rows(parts, offsets, rate):
    top, total, summed = parts
    rows = top.shape[0]
    marks = jnp.arange(rate, dtype=jnp.int32)[None, :, None] == offsets[None, None, :]
    top_full = jnp.where(marks, top[:, None, :], jnp.float32(-1e30)).reshape(rows * rate, -1)
    total_full = jnp.where(marks, total[:, None, :], jnp.float32(0.0)).reshape(rows * rate, -1)
    sum_full = jnp.where(marks[..., None], summed[:, None], jnp.float32(0.0)).reshape(
        rows * rate, summed.shape[1], summed.shape[2]
    )
    return (top_full, total_full, sum_full)


def body(tokens, w_qkv, w_out, norm_gain, w_label, offset_mid, offset_far):
    tok_rows = tokens.shape[0]
    local_heads = offset_mid.shape[0]
    head_size = w_qkv.shape[2] // local_heads
    qkv = jnp.einsum("td,dce->tce", tokens, w_qkv, preferred_element_type=jnp.float32).astype(
        jnp.bfloat16
    )
    qkv = qkv.reshape(tok_rows, 3, local_heads, head_size)
    queries, keys, values = (qkv[:, 0], qkv[:, 1], qkv[:, 2])
    seq_count = lax.axis_size("seq")
    near = attend(queries, keys, values)
    mid_q = select_rows(queries, offset_mid, SPAN)
    mid_kv = jnp.stack(
        [select_rows(keys, offset_mid, SPAN), select_rows(values, offset_mid, SPAN)], axis=0
    )
    mid_rows = mid_kv.shape[1]
    position = (lax.axis_index("seq") + SPAN // 2) % SPAN
    lower_pieces = []
    upper_pieces = []
    for step_back in range(1, SPAN):
        lower_pieces.insert(0, from_behind(mid_kv, "seq", step_back))
        upper_pieces.append(from_behind(mid_kv, "seq", -step_back))
    window = jnp.concatenate(lower_pieces + [mid_kv] + upper_pieces, axis=1)
    gathered = lax.dynamic_slice_in_dim(
        window, (SPAN - 1 - position) * mid_rows, SPAN * mid_rows, 1
    )
    middle = spread_rows(attend(mid_q, gathered[0], gathered[1]), offset_mid, SPAN)
    far_q = select_rows(queries, offset_far, seq_count)
    far_kv = jnp.stack(
        [select_rows(keys, offset_far, seq_count), select_rows(values, offset_far, seq_count)],
        axis=0,
    )
    far_all = lax.all_gather(far_kv, "seq", axis=1, tiled=True)
    distant = spread_rows(attend(far_q, far_all[0], far_all[1]), offset_far, seq_count)
    branches = [near, middle, distant]
    peak = jnp.maximum(jnp.maximum(near[0], middle[0]), distant[0])
    upper = jnp.zeros((tok_rows, local_heads, head_size), jnp.float32)
    lower = jnp.zeros((tok_rows, local_heads), jnp.float32)
    for top, total, summed in branches:
        factor = jnp.exp(top - peak)
        upper = upper + factor[..., None] * summed
        lower = lower + factor * total
    attn = (
        (upper / lower[..., None]).astype(jnp.bfloat16).reshape(tok_rows, local_heads * head_size)
    )
    partial_out = jnp.dot(attn, w_out, preferred_element_type=jnp.float32)
    projected = lax.psum(partial_out.astype(jnp.bfloat16), "head").astype(jnp.float32)
    mixed = tokens.astype(jnp.float32) + projected
    mean_sq = jnp.mean(mixed * mixed, axis=-1)
    scaled = (mixed * norm_gain).astype(jnp.bfloat16)
    product = jnp.dot(scaled, w_label, preferred_element_type=jnp.float32)
    return product / jnp.sqrt(mean_sq + 1e-05)[:, None]


def softmax_parts(queries, keys, values):
    scale = 1.0 / queries.shape[1] ** 0.5
    scores = (
        lax.dot_general(
            queries, keys, (((1,), (1,)), ((), ())), preferred_element_type=jnp.float32
        )
        * scale
    )
    top = jnp.max(scores, axis=-1, keepdims=True)
    weights = jnp.exp(scores - top)
    total = jnp.sum(weights, axis=-1, keepdims=True)
    summed = jnp.dot(weights.astype(jnp.bfloat16), values, preferred_element_type=jnp.float32)
    return summed / total, top + jnp.log(total)


def kernel(
    tok_hbm, wqkv_hbm, wout_hbm, gain_hbm, wlabel_hbm, off_mid, off_far, out_ref,
    tok, wqkv, wout, gain, wlabel, qkv, pair_out, pair_in, ret_o, ret_l, got_o, got_l,
    attn, parts, sib_in, x_out, x_in, log_out, log_in,
    load_sem, w_sem, a2a_send, a2a_recv, o_send, o_recv, l_send, l_recv,
    sib_send, sib_recv, x_send, x_recv, log_send, log_recv,
):
    seq = lax.axis_index("seq")
    head = lax.axis_index("head")
    n_seq = pair_in.shape[0]
    n_head = log_in.shape[0]
    rows = tok.shape[0]
    picked = pair_in.shape[1]
    hd = got_o.shape[2]
    heads = n_seq // 2
    core = lax.rem(head, 2)
    chip = head // 2
    sibling = head + 1 - 2 * core
    across = lax.rem(head + 2, n_head)

    barrier = pltpu.get_barrier_semaphore()
    for d in range(1, n_seq):
        pl.semaphore_signal(
            barrier, inc=1, device_id=(lax.rem(seq + d, n_seq), head), device_id_type=MESH
        )
    for d in range(1, n_head):
        pl.semaphore_signal(
            barrier, inc=1, device_id=(seq, lax.rem(head + d, n_head)), device_id_type=MESH
        )

    wide = wqkv.shape[2]
    halves = qkv.shape[2] // wide
    loads = [pltpu.make_async_copy(tok_hbm, tok, load_sem.at[0])]
    w_loads = []
    for half in range(halves):
        for c in range(3):
            k = half * 3 + c
            w_loads.append(
                pltpu.make_async_copy(
                    wqkv_hbm.at[c, :, pl.ds(half * wide, wide)], wqkv.at[k], w_sem.at[k]
                )
            )
    loads.append(pltpu.make_async_copy(wout_hbm, wout, load_sem.at[1]))
    loads.append(pltpu.make_async_copy(gain_hbm, gain, load_sem.at[2]))
    loads.append(pltpu.make_async_copy(wlabel_hbm, wlabel, load_sem.at[3]))
    loads[0].start()
    for load in w_loads:
        load.start()

    def pair_copy(j):
        return pltpu.make_async_remote_copy(
            src_ref=pair_out.at[j], dst_ref=pair_in.at[seq],
            send_sem=a2a_send.at[j], recv_sem=a2a_recv.at[seq],
            device_id=(j, head), device_id_type=MESH,
        )

    def pair_arrival(i):
        return pltpu.make_async_remote_copy(
            src_ref=pair_out.at[i], dst_ref=pair_in.at[i],
            send_sem=a2a_send.at[i], recv_sem=a2a_recv.at[i],
            device_id=(i, head), device_id_type=MESH,
        )

    both = lax.broadcasted_iota(jnp.int32, (2 * picked, rows), 0)
    is_mid = both < picked
    sel_row = jnp.where(is_mid, both, both - picked) * SPAN
    sel_tok = lax.broadcasted_iota(jnp.int32, (2 * picked, rows), 1)
    loads[0].wait()
    for half in range(halves):
        for c in range(3):
            k = half * 3 + c
            w_loads[k].wait()
            qkv[c, :, half * wide : (half + 1) * wide] = jnp.dot(
                tok[...], wqkv[k], preferred_element_type=jnp.float32
            ).astype(jnp.bfloat16)
        if half == halves - 1:
            for load in loads[1:]:
                load.start()
        if half == 0:
            pl.semaphore_wait(barrier, n_seq + n_head - 2)
        for h in range(half * wide // hd, (half + 1) * wide // hd):
            cols = slice(h * hd, (h + 1) * hd)
            mine = jnp.concatenate([qkv[c, :, cols] for c in range(3)], axis=1)
            spot = sel_row + jnp.where(is_mid, off_mid[h], off_far[h])
            one_hot = (sel_tok == spot).astype(jnp.bfloat16)
            found = jnp.dot(one_hot, mine, preferred_element_type=jnp.float32).astype(
                jnp.bfloat16
            )
            for b in range(2):
                j = b * heads + h
                pair_out[j] = found[b * picked : (b + 1) * picked]

                @pl.when(seq != j)
                def _(j=j):
                    pair_copy(j).start()

    pair_in[seq] = pair_out[seq]

    chunks = x_in.shape[0]
    part = x_in.shape[1]
    width = x_in.shape[2]
    side = 2 * part
    near = []
    for s in range(2):
        first = ((1 - chip) if s == 0 else chip) * side
        place = pl.ds(pl.multiple_of(first, side), side)
        for h in range(heads):
            cols = slice(h * hd, (h + 1) * hd)
            near.append(softmax_parts(qkv[0, place, cols], qkv[1, :, cols], qkv[2, :, cols]))

    for i in range(n_seq):

        @pl.when(seq != i)
        def _(i=i):
            pair_arrival(i).wait_recv()

    everyone = n_seq * picked
    pq, pk, pv = (
        pair_in[:, :, c * hd : (c + 1) * hd].reshape(everyone, hd) for c in range(3)
    )
    o, lse = softmax_parts(pq, pk, pv)
    ret_o[...] = o.astype(jnp.bfloat16).reshape(n_seq, picked, hd)
    per_tile = hd // picked

    def o_copy(i, slot):
        return pltpu.make_async_remote_copy(
            src_ref=ret_o.at[i], dst_ref=got_o.at[slot],
            send_sem=o_send.at[i], recv_sem=o_recv.at[slot],
            device_id=(i, head), device_id_type=MESH,
        )

    def l_copy(i, slot):
        return pltpu.make_async_remote_copy(
            src_ref=ret_l.at[i // per_tile], dst_ref=got_l.at[slot],
            send_sem=l_send.at[i], recv_sem=l_recv.at[slot],
            device_id=(i, head), device_id_type=MESH,
        )

    for i in range(n_seq):

        @pl.when(seq != i)
        def _(i=i):
            o_copy(i, seq).start()

    r0 = lax.broadcasted_iota(jnp.int32, (everyone, everyone), 0)
    r1 = lax.broadcasted_iota(jnp.int32, (everyone, everyone), 1)
    lse_row = jnp.sum(jnp.where(r0 == r1, lse, 0.0), axis=0, keepdims=True)
    for t in range(everyone // hd):
        ret_l[t] = lse_row[:, t * hd : (t + 1) * hd]
    for i in range(n_seq):

        @pl.when(seq != i)
        def _(i=i):
            l_copy(i, seq).start()

    got_o[seq] = ret_o[seq]
    got_l[seq] = ret_l[seq // per_tile]

    base = lax.rem(seq, per_tile) * picked

    def merge(s, first):
        tok_col = lax.broadcasted_iota(jnp.int32, (side, hd), 0) + first
        lane = lax.broadcasted_iota(jnp.int32, (side, hd), 1) - base
        tok_sel = lax.broadcasted_iota(jnp.int32, (side, picked), 0) + first
        row_sel = lax.broadcasted_iota(jnp.int32, (side, picked), 1)
        tok_one = lax.broadcasted_iota(jnp.int32, (side, 1), 0)
        merged = []
        for h in range(heads):
            terms = [near[s * heads + h]]
            marks = [None]
            for b, off in enumerate((off_mid, off_far)):
                j = b * heads + h
                if s == 0:

                    @pl.when(seq != j)
                    def _(j=j):
                        o_copy(j, j).wait_recv()
                        l_copy(j, j).wait_recv()

                spot = off[h]
                hit = lane * SPAN + spot == tok_col
                lse_col = jnp.sum(jnp.where(hit, got_l[j], 0.0), axis=-1, keepdims=True)
                one_hot = (tok_sel == row_sel * SPAN + spot).astype(jnp.bfloat16)
                spread = jnp.dot(one_hot, got_o[j], preferred_element_type=jnp.float32)
                mark = lax.rem(tok_one, SPAN) == spot
                terms.append((spread, jnp.where(mark, lse_col, -1e30)))
                marks.append(mark)
            peak = jnp.maximum(jnp.maximum(terms[0][1], terms[1][1]), terms[2][1])
            upper = jnp.zeros((side, hd), jnp.float32)
            lower = jnp.zeros((side, 1), jnp.float32)
            for (o, lse), mark in zip(terms, marks):
                factor = jnp.exp(lse - peak)
                if mark is not None:
                    factor = jnp.where(mark, factor, 0.0)
                upper = upper + factor * o
                lower = lower + factor
            merged.append((upper / lower).astype(jnp.bfloat16))
        return jnp.concatenate(merged, axis=1)

    def sib_copy(s, n):
        return pltpu.make_async_remote_copy(
            src_ref=parts.at[s, n, 1 - core], dst_ref=sib_in.at[s, n],
            send_sem=sib_send.at[s, n], recv_sem=sib_recv.at[s, n],
            device_id=(seq, sibling), device_id_type=MESH,
        )

    def x_copy(n):
        return pltpu.make_async_remote_copy(
            src_ref=x_out.at[n], dst_ref=x_in.at[n],
            send_sem=x_send.at[n], recv_sem=x_recv.at[n],
            device_id=(seq, across), device_id_type=MESH,
        )

    def pass_on(n):
        sib_copy(0, n).wait_recv()
        x_out[n] = (
            parts[0, n, core].astype(jnp.float32) + sib_in[0, n].astype(jnp.float32)
        ).astype(jnp.bfloat16)
        x_copy(n).start()

    for load in loads[1:]:
        load.wait()
    for s in range(2):
        attn[s] = merge(s, ((1 - chip) if s == 0 else chip) * side)
        for n in range(chunks):
            parts[s, n] = (
                jnp.dot(
                    attn[s], wout[:, n * width : (n + 1) * width],
                    preferred_element_type=jnp.float32,
                )
                .astype(jnp.bfloat16)
                .reshape(2, part, width)
            )
            sib_copy(s, n).start()
            if s == 0 and n > 0:
                pass_on(n - 1)
        if s == 0:
            pass_on(chunks - 1)

    squares = jnp.zeros((part, 1), jnp.float32)
    product = jnp.zeros((part, wlabel.shape[1]), jnp.float32)
    here = pl.ds(pl.multiple_of(head * part, part), part)
    for n in range(chunks):
        cols = slice(n * width, (n + 1) * width)
        sib_copy(1, n).wait_recv()
        x_copy(n).wait_recv()
        summed = parts[1, n, core].astype(jnp.float32) + sib_in[1, n].astype(jnp.float32)
        mixed = tok[here, cols].astype(jnp.float32) + (summed + x_in[n].astype(jnp.float32))
        squares = squares + jnp.sum(mixed * mixed, axis=-1, keepdims=True)
        scaled = (mixed * gain[:, cols]).astype(jnp.bfloat16)
        product = product + jnp.dot(scaled, wlabel[cols, :], preferred_element_type=jnp.float32)
    log_out[...] = (product / jnp.sqrt(squares / tok.shape[1] + 1e-05)).astype(jnp.bfloat16)

    def log_copy(p, slot):
        return pltpu.make_async_remote_copy(
            src_ref=log_out, dst_ref=log_in.at[slot],
            send_sem=log_send.at[p], recv_sem=log_recv.at[slot],
            device_id=(seq, p), device_id_type=MESH,
        )

    for p in range(n_head):

        @pl.when(head != p)
        def _(p=p):
            log_copy(p, head).start()

    log_in[head] = log_out[...]
    for p in range(n_head):

        @pl.when(head != p)
        def _(p=p):
            log_copy(p, p).wait_recv()

        out_ref[p * part : (p + 1) * part, :] = log_in[p]

    for j in range(n_seq):

        @pl.when(seq != j)
        def _(j=j):
            pair_copy(j).wait_send()
            o_copy(j, seq).wait_send()
            l_copy(j, seq).wait_send()

    for n in range(chunks):
        sib_copy(0, n).wait_send()
        sib_copy(1, n).wait_send()
        x_copy(n).wait_send()
    for p in range(n_head):

        @pl.when(head != p)
        def _(p=p):
            log_copy(p, head).wait_send()


def fused_body(n_seq, n_head, tokens, w_qkv, w_out, norm_gain, w_label, offset_mid, offset_far):
    rows, width = tokens.shape
    heads = offset_mid.shape[0]
    own = w_qkv.shape[2]
    hd = own // heads
    classes = w_label.shape[1]
    picked = rows // SPAN
    part = rows // n_head
    chunks = 4
    span = width // chunks
    bf16, f32 = jnp.bfloat16, jnp.float32
    dma = pltpu.SemaphoreType.DMA
    anywhere = pl.BlockSpec(memory_space=pl.ANY)
    scalars = pl.BlockSpec(memory_space=pltpu.SMEM)
    return pl.pallas_call(
        kernel,
        out_shape=pltpu.VMEM((rows, classes), bf16),
        in_specs=[anywhere] * 5 + [scalars] * 2,
        out_specs=pl.BlockSpec(memory_space=pltpu.VMEM),
        scratch_shapes=[
            pltpu.VMEM((rows, width), bf16),
            pltpu.VMEM((6, width, own // 2), bf16),
            pltpu.VMEM((own, width), bf16),
            pltpu.VMEM((1, width), f32),
            pltpu.VMEM((width, classes), bf16),
            pltpu.VMEM((3, rows, own), bf16),
            pltpu.VMEM((n_seq, picked, 3 * hd), bf16),
            pltpu.VMEM((n_seq, picked, 3 * hd), bf16),
            pltpu.VMEM((n_seq, picked, hd), bf16),
            pltpu.VMEM((n_seq * picked // hd, 1, hd), f32),
            pltpu.VMEM((n_seq, picked, hd), bf16),
            pltpu.VMEM((n_seq, 1, hd), f32),
            pltpu.VMEM((2, 2 * part, own), bf16),
            pltpu.VMEM((2, chunks, 2, part, span), bf16),
            pltpu.VMEM((2, chunks, part, span), bf16),
            pltpu.VMEM((chunks, part, span), bf16),
            pltpu.VMEM((chunks, part, span), bf16),
            pltpu.VMEM((part, classes), bf16),
            pltpu.VMEM((n_head, part, classes), bf16),
            dma((4,)), dma((6,)), dma((n_seq,)), dma((n_seq,)),
            dma((n_seq,)), dma((n_seq,)), dma((n_seq,)), dma((n_seq,)),
            dma((2, chunks)), dma((2, chunks)), dma((chunks,)), dma((chunks,)),
            dma((n_head,)), dma((n_head,)),
        ],
        compiler_params=pltpu.CompilerParams(
            collective_id=0, has_side_effects=True, vmem_limit_bytes=56 * 2**20
        ),
    )(
        tokens, jnp.transpose(w_qkv, (1, 0, 2)), w_out, norm_gain[None, :], w_label,
        offset_mid, offset_far,
    ).astype(f32)


def solution(mesh):
    n_seq, n_head = mesh.shape["seq"], mesh.shape["head"]
    run = body
    if n_seq == SPAN and n_head == 4:
        run = functools.partial(fused_body, n_seq, n_head)
    return jax.shard_map(
        run,
        mesh=mesh,
        in_specs=(
            P("seq", None),
            P(None, None, "head"),
            P("head", None),
            P(),
            P(),
            P("head"),
            P("head"),
        ),
        out_specs=P("seq", None),
        check_vma=False,
    )
```

```python
import functools

import jax
import jax.numpy as jnp
from jax import lax
from jax.experimental import pallas as pl
from jax.experimental.pallas import tpu as pltpu
from jax.sharding import PartitionSpec as P

MESH = pl.DeviceIdType.MESH

SPAN = 8


def from_behind(block, axis, distance):
    devices = range(lax.axis_size(axis))
    route = [((i - distance) % len(devices), i) for i in devices]
    return lax.ppermute(block, axis, route)


def attend(queries, keys, values):
    scores = jnp.einsum(
        "rhe,she->hrs", queries, keys, preferred_element_type=jnp.float32
    ) / jnp.sqrt(jnp.float32(queries.shape[2]))
    top = jnp.max(scores, axis=-1)
    weights = jnp.exp(scores - top[..., None])
    total = jnp.sum(weights, axis=-1)
    summed = jnp.einsum(
        "hrs,she->rhe", weights.astype(jnp.bfloat16), values, preferred_element_type=jnp.float32
    )
    return (top.T, total.T, summed)


def select_rows(array, offsets, rate):
    rows = array.shape[0] // rate
    shaped = array.reshape(rows, rate, array.shape[1], array.shape[2])
    marks = jnp.arange(rate, dtype=jnp.int32)[None, :, None] == offsets[None, None, :]
    return jnp.sum(jnp.where(marks[..., None], shaped, jnp.zeros_like(shaped)), axis=1)


def spread_rows(parts, offsets, rate):
    top, total, summed = parts
    rows = top.shape[0]
    marks = jnp.arange(rate, dtype=jnp.int32)[None, :, None] == offsets[None, None, :]
    top_full = jnp.where(marks, top[:, None, :], jnp.float32(-1e30)).reshape(rows * rate, -1)
    total_full = jnp.where(marks, total[:, None, :], jnp.float32(0.0)).reshape(rows * rate, -1)
    sum_full = jnp.where(marks[..., None], summed[:, None], jnp.float32(0.0)).reshape(
        rows * rate, summed.shape[1], summed.shape[2]
    )
    return (top_full, total_full, sum_full)


def body(tokens, w_qkv, w_out, norm_gain, w_label, offset_mid, offset_far):
    tok_rows = tokens.shape[0]
    local_heads = offset_mid.shape[0]
    head_size = w_qkv.shape[2] // local_heads
    qkv = jnp.einsum("td,dce->tce", tokens, w_qkv, preferred_element_type=jnp.float32).astype(
        jnp.bfloat16
    )
    qkv = qkv.reshape(tok_rows, 3, local_heads, head_size)
    queries, keys, values = (qkv[:, 0], qkv[:, 1], qkv[:, 2])
    seq_count = lax.axis_size("seq")
    near = attend(queries, keys, values)
    mid_q = select_rows(queries, offset_mid, SPAN)
    mid_kv = jnp.stack(
        [select_rows(keys, offset_mid, SPAN), select_rows(values, offset_mid, SPAN)], axis=0
    )
    mid_rows = mid_kv.shape[1]
    position = (lax.axis_index("seq") + SPAN // 2) % SPAN
    lower_pieces = []
    upper_pieces = []
    for step_back in range(1, SPAN):
        lower_pieces.insert(0, from_behind(mid_kv, "seq", step_back))
        upper_pieces.append(from_behind(mid_kv, "seq", -step_back))
    window = jnp.concatenate(lower_pieces + [mid_kv] + upper_pieces, axis=1)
    gathered = lax.dynamic_slice_in_dim(
        window, (SPAN - 1 - position) * mid_rows, SPAN * mid_rows, 1
    )
    middle = spread_rows(attend(mid_q, gathered[0], gathered[1]), offset_mid, SPAN)
    far_q = select_rows(queries, offset_far, seq_count)
    far_kv = jnp.stack(
        [select_rows(keys, offset_far, seq_count), select_rows(values, offset_far, seq_count)],
        axis=0,
    )
    far_all = lax.all_gather(far_kv, "seq", axis=1, tiled=True)
    distant = spread_rows(attend(far_q, far_all[0], far_all[1]), offset_far, seq_count)
    branches = [near, middle, distant]
    peak = jnp.maximum(jnp.maximum(near[0], middle[0]), distant[0])
    upper = jnp.zeros((tok_rows, local_heads, head_size), jnp.float32)
    lower = jnp.zeros((tok_rows, local_heads), jnp.float32)
    for top, total, summed in branches:
        factor = jnp.exp(top - peak)
        upper = upper + factor[..., None] * summed
        lower = lower + factor * total
    attn = (
        (upper / lower[..., None]).astype(jnp.bfloat16).reshape(tok_rows, local_heads * head_size)
    )
    partial_out = jnp.dot(attn, w_out, preferred_element_type=jnp.float32)
    projected = lax.psum(partial_out.astype(jnp.bfloat16), "head").astype(jnp.float32)
    mixed = tokens.astype(jnp.float32) + projected
    mean_sq = jnp.mean(mixed * mixed, axis=-1)
    scaled = (mixed * norm_gain).astype(jnp.bfloat16)
    product = jnp.dot(scaled, w_label, preferred_element_type=jnp.float32)
    return product / jnp.sqrt(mean_sq + 1e-05)[:, None]


def softmax_parts(queries, keys, values):
    scale = 1.0 / queries.shape[1] ** 0.5
    scores = (
        lax.dot_general(
            queries, keys, (((1,), (1,)), ((), ())), preferred_element_type=jnp.float32
        )
        * scale
    )
    top = jnp.max(scores, axis=-1, keepdims=True)
    weights = jnp.exp(scores - top)
    total = jnp.sum(weights, axis=-1, keepdims=True)
    summed = jnp.dot(weights.astype(jnp.bfloat16), values, preferred_element_type=jnp.float32)
    return summed / total, top + jnp.log(total)


def kernel(
    tok_hbm, wqkv_hbm, wout_hbm, gain_hbm, wlabel_hbm, off_mid, off_far, out_ref,
    tok, wqkv, wout, gain, wlabel, qkv, pair_out, pair_in, ret_o, ret_l, got_o, got_l,
    attn, parts, sib_in, x_out, x_in, log_out, log_in,
    load_sem, w_sem, a2a_send, a2a_recv, o_send, o_recv, l_send, l_recv,
    sib_send, sib_recv, x_send, x_recv, log_send, log_recv,
):
    seq = lax.axis_index("seq")
    head = lax.axis_index("head")
    n_seq = pair_in.shape[0]
    n_head = log_in.shape[0]
    rows = tok.shape[0]
    picked = pair_in.shape[1]
    hd = got_o.shape[2]
    heads = n_seq // 2
    core = lax.rem(head, 2)
    chip = head // 2
    sibling = head + 1 - 2 * core
    across = lax.rem(head + 2, n_head)

    barrier = pltpu.get_barrier_semaphore()
    for d in range(1, n_seq):
        pl.semaphore_signal(
            barrier, inc=1, device_id=(lax.rem(seq + d, n_seq), head), device_id_type=MESH
        )
    for d in range(1, n_head):
        pl.semaphore_signal(
            barrier, inc=1, device_id=(seq, lax.rem(head + d, n_head)), device_id_type=MESH
        )

    wide = wqkv.shape[2]
    halves = qkv.shape[2] // wide
    loads = [pltpu.make_async_copy(tok_hbm, tok, load_sem.at[0])]
    w_loads = []
    for half in range(halves):
        for c in range(3):
            k = half * 3 + c
            w_loads.append(
                pltpu.make_async_copy(
                    wqkv_hbm.at[c, :, pl.ds(half * wide, wide)], wqkv.at[k], w_sem.at[k]
                )
            )
    loads.append(pltpu.make_async_copy(wout_hbm, wout, load_sem.at[1]))
    loads.append(pltpu.make_async_copy(gain_hbm, gain, load_sem.at[2]))
    loads.append(pltpu.make_async_copy(wlabel_hbm, wlabel, load_sem.at[3]))
    loads[0].start()
    for load in w_loads:
        load.start()

    def pair_copy(j):
        return pltpu.make_async_remote_copy(
            src_ref=pair_out.at[j], dst_ref=pair_in.at[seq],
            send_sem=a2a_send.at[j], recv_sem=a2a_recv.at[seq],
            device_id=(j, head), device_id_type=MESH,
        )

    def pair_arrival(i):
        return pltpu.make_async_remote_copy(
            src_ref=pair_out.at[i], dst_ref=pair_in.at[i],
            send_sem=a2a_send.at[i], recv_sem=a2a_recv.at[i],
            device_id=(i, head), device_id_type=MESH,
        )

    both = lax.broadcasted_iota(jnp.int32, (2 * picked, rows), 0)
    is_mid = both < picked
    sel_row = jnp.where(is_mid, both, both - picked) * SPAN
    sel_tok = lax.broadcasted_iota(jnp.int32, (2 * picked, rows), 1)
    loads[0].wait()
    for half in range(halves):
        for c in range(3):
            k = half * 3 + c
            w_loads[k].wait()
            qkv[c, :, half * wide : (half + 1) * wide] = jnp.dot(
                tok[...], wqkv[k], preferred_element_type=jnp.float32
            ).astype(jnp.bfloat16)
        if half == halves - 1:
            for load in loads[1:]:
                load.start()
        if half == 0:
            pl.semaphore_wait(barrier, n_seq + n_head - 2)
        for h in range(half * wide // hd, (half + 1) * wide // hd):
            cols = slice(h * hd, (h + 1) * hd)
            mine = jnp.concatenate([qkv[c, :, cols] for c in range(3)], axis=1)
            spot = sel_row + jnp.where(is_mid, off_mid[h], off_far[h])
            one_hot = (sel_tok == spot).astype(jnp.bfloat16)
            found = jnp.dot(one_hot, mine, preferred_element_type=jnp.float32).astype(
                jnp.bfloat16
            )
            for b in range(2):
                j = b * heads + h
                pair_out[j] = found[b * picked : (b + 1) * picked]
        ready = heads // halves
        for d in range(2 * ready):
            turn = lax.rem(seq + d, 2 * ready)
            j = turn // ready * heads + half * ready + lax.rem(turn, ready)

            @pl.when(seq != j)
            def _(j=j):
                pair_copy(j).start()

    pair_in[seq] = pair_out[seq]

    chunks = x_in.shape[0]
    part = x_in.shape[1]
    width = x_in.shape[2]
    side = 2 * part
    firsts = ((1 - chip) * side, chip * side)

    def near_rows(s, h):
        place = pl.ds(pl.multiple_of(firsts[s], side), side)
        cols = slice(h * hd, (h + 1) * hd)
        return softmax_parts(qkv[0, place, cols], qkv[1, :, cols], qkv[2, :, cols])

    near = [[near_rows(0, h) for h in range(heads // 2)], []]

    for d in range(1, n_seq):
        pair_arrival(lax.rem(seq + d, n_seq)).wait_recv()

    everyone = n_seq * picked
    pq, pk, pv = (
        pair_in[:, :, c * hd : (c + 1) * hd].reshape(everyone, hd) for c in range(3)
    )
    o, lse = softmax_parts(pq, pk, pv)
    ret_o[...] = o.astype(jnp.bfloat16).reshape(n_seq, picked, hd)
    per_tile = hd // picked

    def o_copy(i, slot):
        return pltpu.make_async_remote_copy(
            src_ref=ret_o.at[i], dst_ref=got_o.at[slot],
            send_sem=o_send.at[i], recv_sem=o_recv.at[slot],
            device_id=(i, head), device_id_type=MESH,
        )

    def l_copy(i, slot):
        return pltpu.make_async_remote_copy(
            src_ref=ret_l.at[i // per_tile], dst_ref=got_l.at[slot],
            send_sem=l_send.at[i], recv_sem=l_recv.at[slot],
            device_id=(i, head), device_id_type=MESH,
        )

    outward = sorted(range(1, n_seq), key=lambda d: abs(2 * d - n_seq))
    for d in outward:
        o_copy(lax.rem(seq + d, n_seq), seq).start()

    r0 = lax.broadcasted_iota(jnp.int32, (everyone, everyone), 0)
    r1 = lax.broadcasted_iota(jnp.int32, (everyone, everyone), 1)
    lse_row = jnp.sum(jnp.where(r0 == r1, lse, 0.0), axis=0, keepdims=True)
    for t in range(everyone // hd):
        ret_l[t] = lse_row[:, t * hd : (t + 1) * hd]
    for d in outward:
        l_copy(lax.rem(seq + d, n_seq), seq).start()

    got_o[seq] = ret_o[seq]
    got_l[seq] = ret_l[seq // per_tile]
    near[0] += [near_rows(0, h) for h in range(heads // 2, heads)]

    base = lax.rem(seq, per_tile) * picked

    def merge(s, first):
        tok_col = lax.broadcasted_iota(jnp.int32, (side, hd), 0) + first
        lane = lax.broadcasted_iota(jnp.int32, (side, hd), 1) - base
        tok_sel = lax.broadcasted_iota(jnp.int32, (side, picked), 0) + first
        row_sel = lax.broadcasted_iota(jnp.int32, (side, picked), 1)
        tok_one = lax.broadcasted_iota(jnp.int32, (side, 1), 0)
        merged = []
        for h in range(heads):
            terms = [near[s][h]]
            marks = [None]
            for b, off in enumerate((off_mid, off_far)):
                j = b * heads + h
                spot = off[h]
                hit = lane * SPAN + spot == tok_col
                lse_col = jnp.sum(jnp.where(hit, got_l[j], 0.0), axis=-1, keepdims=True)
                one_hot = (tok_sel == row_sel * SPAN + spot).astype(jnp.bfloat16)
                spread = jnp.dot(one_hot, got_o[j], preferred_element_type=jnp.float32)
                mark = lax.rem(tok_one, SPAN) == spot
                terms.append((spread, jnp.where(mark, lse_col, -1e30)))
                marks.append(mark)
            peak = jnp.maximum(jnp.maximum(terms[0][1], terms[1][1]), terms[2][1])
            upper = jnp.zeros((side, hd), jnp.float32)
            lower = jnp.zeros((side, 1), jnp.float32)
            for (o, lse), mark in zip(terms, marks):
                factor = jnp.exp(lse - peak)
                if mark is not None:
                    factor = jnp.where(mark, factor, 0.0)
                upper = upper + factor * o
                lower = lower + factor
            merged.append((upper / lower).astype(jnp.bfloat16))
        return jnp.concatenate(merged, axis=1)

    def sib_copy(s, n):
        return pltpu.make_async_remote_copy(
            src_ref=parts.at[s, n, 1 - core], dst_ref=sib_in.at[s, n],
            send_sem=sib_send.at[s, n], recv_sem=sib_recv.at[s, n],
            device_id=(seq, sibling), device_id_type=MESH,
        )

    def x_copy(n):
        return pltpu.make_async_remote_copy(
            src_ref=x_out.at[n], dst_ref=x_in.at[n],
            send_sem=x_send.at[n], recv_sem=x_recv.at[n],
            device_id=(seq, across), device_id_type=MESH,
        )

    def pass_on(n):
        sib_copy(0, n).wait_recv()
        x_out[n] = (
            parts[0, n, core].astype(jnp.float32) + sib_in[0, n].astype(jnp.float32)
        ).astype(jnp.bfloat16)
        x_copy(n).start()

    for load in loads[1:]:
        load.wait()
    for d in range(1, n_seq):
        j = lax.rem(seq + d, n_seq)
        o_copy(j, j).wait_recv()
        l_copy(j, j).wait_recv()
    for s in range(2):
        if s == 1:
            near[1] = [near_rows(1, h) for h in range(heads)]
        attn[s] = merge(s, firsts[s])
        for n in range(chunks):
            parts[s, n] = (
                jnp.dot(
                    attn[s], wout[:, n * width : (n + 1) * width],
                    preferred_element_type=jnp.float32,
                )
                .astype(jnp.bfloat16)
                .reshape(2, part, width)
            )
            sib_copy(s, n).start()
            if s == 0 and n > 0:
                pass_on(n - 1)
        if s == 0:
            pass_on(chunks - 1)

    squares = jnp.zeros((part, 1), jnp.float32)
    product = jnp.zeros((part, wlabel.shape[1]), jnp.float32)
    here = pl.ds(pl.multiple_of(head * part, part), part)
    for n in range(chunks):
        cols = slice(n * width, (n + 1) * width)
        sib_copy(1, n).wait_recv()
        x_copy(n).wait_recv()
        summed = parts[1, n, core].astype(jnp.float32) + sib_in[1, n].astype(jnp.float32)
        mixed = tok[here, cols].astype(jnp.float32) + (summed + x_in[n].astype(jnp.float32))
        squares = squares + jnp.sum(mixed * mixed, axis=-1, keepdims=True)
        scaled = (mixed * gain[:, cols]).astype(jnp.bfloat16)
        product = product + jnp.dot(scaled, wlabel[cols, :], preferred_element_type=jnp.float32)
    log_out[...] = (product / jnp.sqrt(squares / tok.shape[1] + 1e-05)).astype(jnp.bfloat16)

    def log_copy(p, slot):
        return pltpu.make_async_remote_copy(
            src_ref=log_out, dst_ref=log_in.at[slot],
            send_sem=log_send.at[p], recv_sem=log_recv.at[slot],
            device_id=(seq, p), device_id_type=MESH,
        )

    for d in (2, 1, 3):
        log_copy(lax.rem(head + d, n_head), head).start()
    log_in[head] = log_out[...]
    for d in range(1, n_head):
        p = lax.rem(head + d, n_head)
        log_copy(p, p).wait_recv()
    for p in range(n_head):
        out_ref[p * part : (p + 1) * part, :] = log_in[p]

    for d in range(1, n_seq):
        j = lax.rem(seq + d, n_seq)
        pair_copy(j).wait_send()
        o_copy(j, seq).wait_send()
        l_copy(j, seq).wait_send()

    for n in range(chunks):
        sib_copy(0, n).wait_send()
        sib_copy(1, n).wait_send()
        x_copy(n).wait_send()
    for d in range(1, n_head):
        log_copy(lax.rem(head + d, n_head), head).wait_send()


def fused_body(n_seq, n_head, tokens, w_qkv, w_out, norm_gain, w_label, offset_mid, offset_far):
    rows, width = tokens.shape
    heads = offset_mid.shape[0]
    own = w_qkv.shape[2]
    hd = own // heads
    classes = w_label.shape[1]
    picked = rows // SPAN
    part = rows // n_head
    chunks = 4
    span = width // chunks
    bf16, f32 = jnp.bfloat16, jnp.float32
    dma = pltpu.SemaphoreType.DMA
    anywhere = pl.BlockSpec(memory_space=pl.ANY)
    scalars = pl.BlockSpec(memory_space=pltpu.SMEM)
    return pl.pallas_call(
        kernel,
        out_shape=pltpu.VMEM((rows, classes), bf16),
        in_specs=[anywhere] * 5 + [scalars] * 2,
        out_specs=pl.BlockSpec(memory_space=pltpu.VMEM),
        scratch_shapes=[
            pltpu.VMEM((rows, width), bf16),
            pltpu.VMEM((6, width, own // 2), bf16),
            pltpu.VMEM((own, width), bf16),
            pltpu.VMEM((1, width), f32),
            pltpu.VMEM((width, classes), bf16),
            pltpu.VMEM((3, rows, own), bf16),
            pltpu.VMEM((n_seq, picked, 3 * hd), bf16),
            pltpu.VMEM((n_seq, picked, 3 * hd), bf16),
            pltpu.VMEM((n_seq, picked, hd), bf16),
            pltpu.VMEM((n_seq * picked // hd, 1, hd), f32),
            pltpu.VMEM((n_seq, picked, hd), bf16),
            pltpu.VMEM((n_seq, 1, hd), f32),
            pltpu.VMEM((2, 2 * part, own), bf16),
            pltpu.VMEM((2, chunks, 2, part, span), bf16),
            pltpu.VMEM((2, chunks, part, span), bf16),
            pltpu.VMEM((chunks, part, span), bf16),
            pltpu.VMEM((chunks, part, span), bf16),
            pltpu.VMEM((part, classes), bf16),
            pltpu.VMEM((n_head, part, classes), bf16),
            dma((4,)), dma((6,)), dma((n_seq,)), dma((n_seq,)),
            dma((n_seq,)), dma((n_seq,)), dma((n_seq,)), dma((n_seq,)),
            dma((2, chunks)), dma((2, chunks)), dma((chunks,)), dma((chunks,)),
            dma((n_head,)), dma((n_head,)),
        ],
        compiler_params=pltpu.CompilerParams(
            collective_id=0, has_side_effects=True, vmem_limit_bytes=56 * 2**20
        ),
    )(
        tokens, jnp.transpose(w_qkv, (1, 0, 2)), w_out, norm_gain[None, :], w_label,
        offset_mid, offset_far,
    ).astype(f32)


def solution(mesh):
    n_seq, n_head = mesh.shape["seq"], mesh.shape["head"]
    run = body
    if n_seq == SPAN and n_head == 4:
        run = functools.partial(fused_body, n_seq, n_head)
    return jax.shard_map(
        run,
        mesh=mesh,
        in_specs=(
            P("seq", None),
            P(None, None, "head"),
            P("head", None),
            P(),
            P(),
            P("head"),
            P("head"),
        ),
        out_specs=P("seq", None),
        check_vma=False,
    )
```

```python
import functools

import jax
import jax.numpy as jnp
from jax import lax
from jax.experimental import pallas as pl
from jax.experimental.pallas import tpu as pltpu
from jax.sharding import PartitionSpec as P

MESH = pl.DeviceIdType.MESH

SPAN = 8


def from_behind(block, axis, distance):
    devices = range(lax.axis_size(axis))
    route = [((i - distance) % len(devices), i) for i in devices]
    return lax.ppermute(block, axis, route)


def attend(queries, keys, values):
    scores = jnp.einsum(
        "rhe,she->hrs", queries, keys, preferred_element_type=jnp.float32
    ) / jnp.sqrt(jnp.float32(queries.shape[2]))
    top = jnp.max(scores, axis=-1)
    weights = jnp.exp(scores - top[..., None])
    total = jnp.sum(weights, axis=-1)
    summed = jnp.einsum(
        "hrs,she->rhe", weights.astype(jnp.bfloat16), values, preferred_element_type=jnp.float32
    )
    return (top.T, total.T, summed)


def select_rows(array, offsets, rate):
    rows = array.shape[0] // rate
    shaped = array.reshape(rows, rate, array.shape[1], array.shape[2])
    marks = jnp.arange(rate, dtype=jnp.int32)[None, :, None] == offsets[None, None, :]
    return jnp.sum(jnp.where(marks[..., None], shaped, jnp.zeros_like(shaped)), axis=1)


def spread_rows(parts, offsets, rate):
    top, total, summed = parts
    rows = top.shape[0]
    marks = jnp.arange(rate, dtype=jnp.int32)[None, :, None] == offsets[None, None, :]
    top_full = jnp.where(marks, top[:, None, :], jnp.float32(-1e30)).reshape(rows * rate, -1)
    total_full = jnp.where(marks, total[:, None, :], jnp.float32(0.0)).reshape(rows * rate, -1)
    sum_full = jnp.where(marks[..., None], summed[:, None], jnp.float32(0.0)).reshape(
        rows * rate, summed.shape[1], summed.shape[2]
    )
    return (top_full, total_full, sum_full)


def body(tokens, w_qkv, w_out, norm_gain, w_label, offset_mid, offset_far):
    tok_rows = tokens.shape[0]
    local_heads = offset_mid.shape[0]
    head_size = w_qkv.shape[2] // local_heads
    qkv = jnp.einsum("td,dce->tce", tokens, w_qkv, preferred_element_type=jnp.float32).astype(
        jnp.bfloat16
    )
    qkv = qkv.reshape(tok_rows, 3, local_heads, head_size)
    queries, keys, values = (qkv[:, 0], qkv[:, 1], qkv[:, 2])
    seq_count = lax.axis_size("seq")
    near = attend(queries, keys, values)
    mid_q = select_rows(queries, offset_mid, SPAN)
    mid_kv = jnp.stack(
        [select_rows(keys, offset_mid, SPAN), select_rows(values, offset_mid, SPAN)], axis=0
    )
    mid_rows = mid_kv.shape[1]
    position = (lax.axis_index("seq") + SPAN // 2) % SPAN
    lower_pieces = []
    upper_pieces = []
    for step_back in range(1, SPAN):
        lower_pieces.insert(0, from_behind(mid_kv, "seq", step_back))
        upper_pieces.append(from_behind(mid_kv, "seq", -step_back))
    window = jnp.concatenate(lower_pieces + [mid_kv] + upper_pieces, axis=1)
    gathered = lax.dynamic_slice_in_dim(
        window, (SPAN - 1 - position) * mid_rows, SPAN * mid_rows, 1
    )
    middle = spread_rows(attend(mid_q, gathered[0], gathered[1]), offset_mid, SPAN)
    far_q = select_rows(queries, offset_far, seq_count)
    far_kv = jnp.stack(
        [select_rows(keys, offset_far, seq_count), select_rows(values, offset_far, seq_count)],
        axis=0,
    )
    far_all = lax.all_gather(far_kv, "seq", axis=1, tiled=True)
    distant = spread_rows(attend(far_q, far_all[0], far_all[1]), offset_far, seq_count)
    branches = [near, middle, distant]
    peak = jnp.maximum(jnp.maximum(near[0], middle[0]), distant[0])
    upper = jnp.zeros((tok_rows, local_heads, head_size), jnp.float32)
    lower = jnp.zeros((tok_rows, local_heads), jnp.float32)
    for top, total, summed in branches:
        factor = jnp.exp(top - peak)
        upper = upper + factor[..., None] * summed
        lower = lower + factor * total
    attn = (
        (upper / lower[..., None]).astype(jnp.bfloat16).reshape(tok_rows, local_heads * head_size)
    )
    partial_out = jnp.dot(attn, w_out, preferred_element_type=jnp.float32)
    projected = lax.psum(partial_out.astype(jnp.bfloat16), "head").astype(jnp.float32)
    mixed = tokens.astype(jnp.float32) + projected
    mean_sq = jnp.mean(mixed * mixed, axis=-1)
    scaled = (mixed * norm_gain).astype(jnp.bfloat16)
    product = jnp.dot(scaled, w_label, preferred_element_type=jnp.float32)
    return product / jnp.sqrt(mean_sq + 1e-05)[:, None]


def softmax_parts(queries, keys, values):
    scale = 1.0 / queries.shape[1] ** 0.5
    scores = (
        lax.dot_general(
            queries, keys, (((1,), (1,)), ((), ())), preferred_element_type=jnp.float32
        )
        * scale
    )
    top = jnp.max(scores, axis=-1, keepdims=True)
    weights = jnp.exp(scores - top)
    total = jnp.sum(weights, axis=-1, keepdims=True)
    summed = jnp.dot(weights.astype(jnp.bfloat16), values, preferred_element_type=jnp.float32)
    return summed / total, top + jnp.log(total)


def repeat(first, last, step):
    def run(i, carry):
        step(i)
        return carry

    lax.fori_loop(first, last, run, 0)


def kernel(
    tok_hbm, wqkv_hbm, wout_hbm, gain_hbm, wlabel_hbm, off_mid, off_far, out_ref,
    tok, wqkv, wout, gain, wlabel, qkv, near_o, near_l, pair_out, pair_in, ret_o, ret_l, got_o, got_l,
    attn, parts, sib_in, x_out, x_in, log_out, log_in,
    load_sem, w_sem, a2a_send, a2a_recv, o_send, o_recv, l_send, l_recv,
    sib_send, sib_recv, x_send, x_recv, log_send, log_recv,
):
    seq = lax.axis_index("seq")
    head = lax.axis_index("head")
    n_seq = pair_in.shape[0]
    n_head = log_in.shape[0]
    rows = tok.shape[0]
    picked = pair_in.shape[1]
    hd = got_o.shape[2]
    heads = n_seq // 2
    core = lax.rem(head, 2)
    chip = head // 2
    sibling = head + 1 - 2 * core
    across = lax.rem(head + 2, n_head)

    barrier = pltpu.get_barrier_semaphore()
    for d in range(1, n_seq):
        pl.semaphore_signal(
            barrier, inc=1, device_id=(lax.rem(seq + d, n_seq), head), device_id_type=MESH
        )
    for d in range(1, n_head):
        pl.semaphore_signal(
            barrier, inc=1, device_id=(seq, lax.rem(head + d, n_head)), device_id_type=MESH
        )

    wide = wqkv.shape[2]
    halves = wqkv.shape[0] // 3
    ready = heads // halves
    loads = [
        pltpu.make_async_copy(tok_hbm, tok, load_sem.at[0]),
        pltpu.make_async_copy(wout_hbm, wout, load_sem.at[1]),
        pltpu.make_async_copy(gain_hbm, gain, load_sem.at[2]),
        pltpu.make_async_copy(wlabel_hbm, wlabel, load_sem.at[3]),
    ]

    def w_load(half, c):
        cols = pl.ds(pl.multiple_of(half * wide, wide), wide)
        k = half * 3 + c
        return pltpu.make_async_copy(wqkv_hbm.at[c, :, cols], wqkv.at[k], w_sem.at[k])

    loads[0].start()
    for half in range(halves):
        for c in range(3):
            w_load(half, c).start()

    def pair_copy(j):
        return pltpu.make_async_remote_copy(
            src_ref=pair_out.at[j], dst_ref=pair_in.at[seq],
            send_sem=a2a_send.at[j], recv_sem=a2a_recv.at[seq],
            device_id=(j, head), device_id_type=MESH,
        )

    def pair_arrival(i):
        return pltpu.make_async_remote_copy(
            src_ref=pair_out.at[i], dst_ref=pair_in.at[i],
            send_sem=a2a_send.at[i], recv_sem=a2a_recv.at[i],
            device_id=(i, head), device_id_type=MESH,
        )

    both = lax.broadcasted_iota(jnp.int32, (2 * picked, rows), 0)
    is_mid = both < picked
    sel_row = jnp.where(is_mid, both, both - picked) * SPAN
    sel_tok = lax.broadcasted_iota(jnp.int32, (2 * picked, rows), 1)
    loads[0].wait()

    def project_half(half):
        def project(c):
            w_load(half, c).wait()
            result = jnp.dot(
                tok[...], wqkv[half * 3 + c], preferred_element_type=jnp.float32
            ).astype(jnp.bfloat16)
            for i in range(ready):
                qkv[c, half * ready + i] = result[:, i * hd : (i + 1) * hd]

        repeat(0, 3, project)

        @pl.when(half == 0)
        def _():
            pl.semaphore_wait(barrier, n_seq + n_head - 2)

        for i in range(ready):
            h = half * ready + i
            mine = jnp.concatenate([qkv[c, h] for c in range(3)], axis=1)
            spot = sel_row + jnp.where(is_mid, off_mid[h], off_far[h])
            one_hot = (sel_tok == spot).astype(jnp.bfloat16)
            found = jnp.dot(one_hot, mine, preferred_element_type=jnp.float32).astype(
                jnp.bfloat16
            )
            for b in range(2):
                pair_out[b * heads + h] = found[b * picked : (b + 1) * picked]

        def send(d):
            turn = lax.rem(seq + d, 2 * ready)
            j = turn // ready * heads + half * ready + lax.rem(turn, ready)

            @pl.when(seq != j)
            def _():
                pair_copy(j).start()

        repeat(0, 2 * ready, send)

    repeat(0, halves, project_half)
    for load in loads[1:]:
        load.start()
    pair_in[seq] = pair_out[seq]

    chunks = x_in.shape[0]
    part = x_in.shape[1]
    width = x_in.shape[2]
    side = 2 * part
    def near_head(h):
        o, lse = softmax_parts(qkv[0, h], qkv[1, h], qkv[2, h])
        near_o[h] = o
        near_l[h] = lse

    repeat(0, heads, near_head)

    repeat(1, n_seq, lambda d: pair_arrival(lax.rem(seq + d, n_seq)).wait_recv())

    everyone = n_seq * picked
    pq, pk, pv = (
        pair_in[:, :, c * hd : (c + 1) * hd].reshape(everyone, hd) for c in range(3)
    )
    o, lse = softmax_parts(pq, pk, pv)
    ret_o[...] = o.astype(jnp.bfloat16).reshape(n_seq, picked, hd)
    per_tile = hd // picked

    def o_copy(i, slot):
        return pltpu.make_async_remote_copy(
            src_ref=ret_o.at[i], dst_ref=got_o.at[slot],
            send_sem=o_send.at[i], recv_sem=o_recv.at[slot],
            device_id=(i, head), device_id_type=MESH,
        )

    def l_copy(i, slot):
        return pltpu.make_async_remote_copy(
            src_ref=ret_l.at[i // per_tile], dst_ref=got_l.at[slot],
            send_sem=l_send.at[i], recv_sem=l_recv.at[slot],
            device_id=(i, head), device_id_type=MESH,
        )

    repeat(1, n_seq, lambda d: o_copy(lax.rem(seq + d, n_seq), seq).start())

    r0 = lax.broadcasted_iota(jnp.int32, (everyone, everyone), 0)
    r1 = lax.broadcasted_iota(jnp.int32, (everyone, everyone), 1)
    lse_row = jnp.sum(jnp.where(r0 == r1, lse, 0.0), axis=0, keepdims=True)
    for t in range(everyone // hd):
        ret_l[t] = lse_row[:, t * hd : (t + 1) * hd]
    repeat(1, n_seq, lambda d: l_copy(lax.rem(seq + d, n_seq), seq).start())

    got_o[seq] = ret_o[seq]
    got_l[seq] = ret_l[seq // per_tile]

    base = lax.rem(seq, per_tile) * picked

    def merge(s, first, h):
        tok_col = lax.broadcasted_iota(jnp.int32, (side, hd), 0) + first
        lane = lax.broadcasted_iota(jnp.int32, (side, hd), 1) - base
        tok_sel = lax.broadcasted_iota(jnp.int32, (side, picked), 0) + first
        row_sel = lax.broadcasted_iota(jnp.int32, (side, picked), 1)
        tok_one = lax.broadcasted_iota(jnp.int32, (side, 1), 0)
        place = pl.ds(pl.multiple_of(first, side), side)
        terms = [(near_o[h, place, :], near_l[h, place, :])]
        marks = [None]
        for b, off in enumerate((off_mid, off_far)):
            j = b * heads + h
            spot = off[h]
            hit = lane * SPAN + spot == tok_col
            lse_col = jnp.sum(jnp.where(hit, got_l[j], 0.0), axis=-1, keepdims=True)
            one_hot = (tok_sel == row_sel * SPAN + spot).astype(jnp.bfloat16)
            spread = jnp.dot(one_hot, got_o[j], preferred_element_type=jnp.float32)
            mark = lax.rem(tok_one, SPAN) == spot
            terms.append((spread, jnp.where(mark, lse_col, -1e30)))
            marks.append(mark)
        peak = jnp.maximum(jnp.maximum(terms[0][1], terms[1][1]), terms[2][1])
        upper = jnp.zeros((side, hd), jnp.float32)
        lower = jnp.zeros((side, 1), jnp.float32)
        for (o, lse), mark in zip(terms, marks):
            factor = jnp.exp(lse - peak)
            if mark is not None:
                factor = jnp.where(mark, factor, 0.0)
            upper = upper + factor * o
            lower = lower + factor
        return (upper / lower).astype(jnp.bfloat16)

    def sib_copy(s, n):
        return pltpu.make_async_remote_copy(
            src_ref=parts.at[s, n, 1 - core], dst_ref=sib_in.at[s, n],
            send_sem=sib_send.at[s, n], recv_sem=sib_recv.at[s, n],
            device_id=(seq, sibling), device_id_type=MESH,
        )

    def x_copy(n):
        return pltpu.make_async_remote_copy(
            src_ref=x_out.at[n], dst_ref=x_in.at[n],
            send_sem=x_send.at[n], recv_sem=x_recv.at[n],
            device_id=(seq, across), device_id_type=MESH,
        )

    def pass_on(n):
        sib_copy(0, n).wait_recv()
        x_out[n] = (
            parts[0, n, core].astype(jnp.float32) + sib_in[0, n].astype(jnp.float32)
        ).astype(jnp.bfloat16)
        x_copy(n).start()

    for load in loads[1:]:
        load.wait()
    def returned(d):
        j = lax.rem(seq + d, n_seq)
        o_copy(j, j).wait_recv()
        l_copy(j, j).wait_recv()

    repeat(1, n_seq, returned)

    def project_side(s):
        first = lax.rem(1 - chip + s, 2) * side

        def merge_pair(g):
            for i in range(2):
                h = 2 * g + i
                attn[s, :, pl.ds(pl.multiple_of(h * hd, hd), hd)] = merge(s, first, h)

        repeat(0, heads // 2, merge_pair)

        def project_out(n):
            cols = pl.ds(pl.multiple_of(n * width, width), width)
            parts[s, n] = (
                jnp.dot(attn[s], wout[:, cols], preferred_element_type=jnp.float32)
                .astype(jnp.bfloat16)
                .reshape(2, part, width)
            )
            sib_copy(s, n).start()

            @pl.when((s == 0) & (n > 0))
            def _():
                pass_on(n - 1)

        repeat(0, chunks, project_out)

        @pl.when(s == 0)
        def _():
            pass_on(chunks - 1)

    repeat(0, 2, project_side)

    here = pl.ds(pl.multiple_of(head * part, part), part)

    def finish(n, carry):
        squares, product = carry
        cols = pl.ds(pl.multiple_of(n * width, width), width)
        sib_copy(1, n).wait_recv()
        x_copy(n).wait_recv()
        summed = parts[1, n, core].astype(jnp.float32) + sib_in[1, n].astype(jnp.float32)
        mixed = tok[here, cols].astype(jnp.float32) + (summed + x_in[n].astype(jnp.float32))
        squares = squares + jnp.sum(mixed * mixed, axis=-1, keepdims=True)
        scaled = (mixed * gain[:, cols]).astype(jnp.bfloat16)
        product = product + jnp.dot(scaled, wlabel[cols, :], preferred_element_type=jnp.float32)
        return squares, product

    squares, product = lax.fori_loop(
        0,
        chunks,
        finish,
        (jnp.zeros((part, 1), jnp.float32), jnp.zeros((part, wlabel.shape[1]), jnp.float32)),
    )
    log_out[...] = (product / jnp.sqrt(squares / tok.shape[1] + 1e-05)).astype(jnp.bfloat16)

    def log_copy(p, slot):
        return pltpu.make_async_remote_copy(
            src_ref=log_out, dst_ref=log_in.at[slot],
            send_sem=log_send.at[p], recv_sem=log_recv.at[slot],
            device_id=(seq, p), device_id_type=MESH,
        )

    for d in (2, 1, 3):
        log_copy(lax.rem(head + d, n_head), head).start()
    log_in[head] = log_out[...]
    for d in range(1, n_head):
        p = lax.rem(head + d, n_head)
        log_copy(p, p).wait_recv()
    for p in range(n_head):
        out_ref[p * part : (p + 1) * part, :] = log_in[p]

    def sent(d):
        j = lax.rem(seq + d, n_seq)
        pair_copy(j).wait_send()
        o_copy(j, seq).wait_send()
        l_copy(j, seq).wait_send()

    repeat(1, n_seq, sent)

    def sent_parts(n):
        sib_copy(0, n).wait_send()
        sib_copy(1, n).wait_send()
        x_copy(n).wait_send()

    repeat(0, chunks, sent_parts)
    for d in range(1, n_head):
        log_copy(lax.rem(head + d, n_head), head).wait_send()


def fused_body(n_seq, n_head, tokens, w_qkv, w_out, norm_gain, w_label, offset_mid, offset_far):
    rows, width = tokens.shape
    heads = offset_mid.shape[0]
    own = w_qkv.shape[2]
    hd = own // heads
    classes = w_label.shape[1]
    picked = rows // SPAN
    part = rows // n_head
    chunks = 4
    span = width // chunks
    bf16, f32 = jnp.bfloat16, jnp.float32
    dma = pltpu.SemaphoreType.DMA
    anywhere = pl.BlockSpec(memory_space=pl.ANY)
    scalars = pl.BlockSpec(memory_space=pltpu.SMEM)
    return pl.pallas_call(
        kernel,
        out_shape=pltpu.VMEM((rows, classes), bf16),
        in_specs=[anywhere] * 5 + [scalars] * 2,
        out_specs=pl.BlockSpec(memory_space=pltpu.VMEM),
        scratch_shapes=[
            pltpu.VMEM((rows, width), bf16),
            pltpu.VMEM((6, width, own // 2), bf16),
            pltpu.VMEM((own, width), bf16),
            pltpu.VMEM((1, width), f32),
            pltpu.VMEM((width, classes), bf16),
            pltpu.VMEM((3, heads, rows, hd), bf16),
            pltpu.VMEM((heads, rows, hd), f32),
            pltpu.VMEM((heads, rows, 1), f32),
            pltpu.VMEM((n_seq, picked, 3 * hd), bf16),
            pltpu.VMEM((n_seq, picked, 3 * hd), bf16),
            pltpu.VMEM((n_seq, picked, hd), bf16),
            pltpu.VMEM((n_seq * picked // hd, 1, hd), f32),
            pltpu.VMEM((n_seq, picked, hd), bf16),
            pltpu.VMEM((n_seq, 1, hd), f32),
            pltpu.VMEM((2, 2 * part, own), bf16),
            pltpu.VMEM((2, chunks, 2, part, span), bf16),
            pltpu.VMEM((2, chunks, part, span), bf16),
            pltpu.VMEM((chunks, part, span), bf16),
            pltpu.VMEM((chunks, part, span), bf16),
            pltpu.VMEM((part, classes), bf16),
            pltpu.VMEM((n_head, part, classes), bf16),
            dma((4,)), dma((6,)), dma((n_seq,)), dma((n_seq,)),
            dma((n_seq,)), dma((n_seq,)), dma((n_seq,)), dma((n_seq,)),
            dma((2, chunks)), dma((2, chunks)), dma((chunks,)), dma((chunks,)),
            dma((n_head,)), dma((n_head,)),
        ],
        compiler_params=pltpu.CompilerParams(
            collective_id=0, has_side_effects=True, vmem_limit_bytes=56 * 2**20
        ),
    )(
        tokens, jnp.transpose(w_qkv, (1, 0, 2)), w_out, norm_gain[None, :], w_label,
        offset_mid, offset_far,
    ).astype(f32)


def solution(mesh):
    n_seq, n_head = mesh.shape["seq"], mesh.shape["head"]
    run = body
    if n_seq == SPAN and n_head == 4:
        run = functools.partial(fused_body, n_seq, n_head)
    return jax.shard_map(
        run,
        mesh=mesh,
        in_specs=(
            P("seq", None),
            P(None, None, "head"),
            P("head", None),
            P(),
            P(),
            P("head"),
            P("head"),
        ),
        out_specs=P("seq", None),
        check_vma=False,
    )
```

```python
import functools

import jax
import jax.numpy as jnp
from jax import lax
from jax.experimental import pallas as pl
from jax.experimental.pallas import tpu as pltpu
from jax.sharding import PartitionSpec as P

MESH = pl.DeviceIdType.MESH

SPAN = 8


def from_behind(block, axis, distance):
    devices = range(lax.axis_size(axis))
    route = [((i - distance) % len(devices), i) for i in devices]
    return lax.ppermute(block, axis, route)


def attend(queries, keys, values):
    scores = jnp.einsum(
        "rhe,she->hrs", queries, keys, preferred_element_type=jnp.float32
    ) / jnp.sqrt(jnp.float32(queries.shape[2]))
    top = jnp.max(scores, axis=-1)
    weights = jnp.exp(scores - top[..., None])
    total = jnp.sum(weights, axis=-1)
    summed = jnp.einsum(
        "hrs,she->rhe", weights.astype(jnp.bfloat16), values, preferred_element_type=jnp.float32
    )
    return (top.T, total.T, summed)


def select_rows(array, offsets, rate):
    rows = array.shape[0] // rate
    shaped = array.reshape(rows, rate, array.shape[1], array.shape[2])
    marks = jnp.arange(rate, dtype=jnp.int32)[None, :, None] == offsets[None, None, :]
    return jnp.sum(jnp.where(marks[..., None], shaped, jnp.zeros_like(shaped)), axis=1)


def spread_rows(parts, offsets, rate):
    top, total, summed = parts
    rows = top.shape[0]
    marks = jnp.arange(rate, dtype=jnp.int32)[None, :, None] == offsets[None, None, :]
    top_full = jnp.where(marks, top[:, None, :], jnp.float32(-1e30)).reshape(rows * rate, -1)
    total_full = jnp.where(marks, total[:, None, :], jnp.float32(0.0)).reshape(rows * rate, -1)
    sum_full = jnp.where(marks[..., None], summed[:, None], jnp.float32(0.0)).reshape(
        rows * rate, summed.shape[1], summed.shape[2]
    )
    return (top_full, total_full, sum_full)


def body(tokens, w_qkv, w_out, norm_gain, w_label, offset_mid, offset_far):
    tok_rows = tokens.shape[0]
    local_heads = offset_mid.shape[0]
    head_size = w_qkv.shape[2] // local_heads
    qkv = jnp.einsum("td,dce->tce", tokens, w_qkv, preferred_element_type=jnp.float32).astype(
        jnp.bfloat16
    )
    qkv = qkv.reshape(tok_rows, 3, local_heads, head_size)
    queries, keys, values = (qkv[:, 0], qkv[:, 1], qkv[:, 2])
    seq_count = lax.axis_size("seq")
    near = attend(queries, keys, values)
    mid_q = select_rows(queries, offset_mid, SPAN)
    mid_kv = jnp.stack(
        [select_rows(keys, offset_mid, SPAN), select_rows(values, offset_mid, SPAN)], axis=0
    )
    mid_rows = mid_kv.shape[1]
    position = (lax.axis_index("seq") + SPAN // 2) % SPAN
    lower_pieces = []
    upper_pieces = []
    for step_back in range(1, SPAN):
        lower_pieces.insert(0, from_behind(mid_kv, "seq", step_back))
        upper_pieces.append(from_behind(mid_kv, "seq", -step_back))
    window = jnp.concatenate(lower_pieces + [mid_kv] + upper_pieces, axis=1)
    gathered = lax.dynamic_slice_in_dim(
        window, (SPAN - 1 - position) * mid_rows, SPAN * mid_rows, 1
    )
    middle = spread_rows(attend(mid_q, gathered[0], gathered[1]), offset_mid, SPAN)
    far_q = select_rows(queries, offset_far, seq_count)
    far_kv = jnp.stack(
        [select_rows(keys, offset_far, seq_count), select_rows(values, offset_far, seq_count)],
        axis=0,
    )
    far_all = lax.all_gather(far_kv, "seq", axis=1, tiled=True)
    distant = spread_rows(attend(far_q, far_all[0], far_all[1]), offset_far, seq_count)
    branches = [near, middle, distant]
    peak = jnp.maximum(jnp.maximum(near[0], middle[0]), distant[0])
    upper = jnp.zeros((tok_rows, local_heads, head_size), jnp.float32)
    lower = jnp.zeros((tok_rows, local_heads), jnp.float32)
    for top, total, summed in branches:
        factor = jnp.exp(top - peak)
        upper = upper + factor[..., None] * summed
        lower = lower + factor * total
    attn = (
        (upper / lower[..., None]).astype(jnp.bfloat16).reshape(tok_rows, local_heads * head_size)
    )
    partial_out = jnp.dot(attn, w_out, preferred_element_type=jnp.float32)
    projected = lax.psum(partial_out.astype(jnp.bfloat16), "head").astype(jnp.float32)
    mixed = tokens.astype(jnp.float32) + projected
    mean_sq = jnp.mean(mixed * mixed, axis=-1)
    scaled = (mixed * norm_gain).astype(jnp.bfloat16)
    product = jnp.dot(scaled, w_label, preferred_element_type=jnp.float32)
    return product / jnp.sqrt(mean_sq + 1e-05)[:, None]


def softmax_parts(queries, keys, values):
    scale = 1.0 / queries.shape[1] ** 0.5
    scores = (
        lax.dot_general(
            queries, keys, (((1,), (1,)), ((), ())), preferred_element_type=jnp.float32
        )
        * scale
    )
    top = jnp.max(scores, axis=-1, keepdims=True)
    weights = jnp.exp(scores - top)
    total = jnp.sum(weights, axis=-1, keepdims=True)
    summed = jnp.dot(weights.astype(jnp.bfloat16), values, preferred_element_type=jnp.float32)
    return summed / total, top + jnp.log(total)


def repeat(first, last, step):
    def run(i, carry):
        step(i)
        return carry

    lax.fori_loop(first, last, run, 0)


def kernel(
    tok_hbm, wqkv_hbm, wout_hbm, gain_hbm, wlabel_hbm, off_mid, off_far, out_ref,
    tok, wqkv, wout, gain, wlabel, qkv, near_o, near_l, pair_out, pair_in, ret_o, ret_l, got_o, got_l,
    attn, parts, sib_in, x_out, x_in, log_out, log_in,
    load_sem, w_sem, a2a_send, a2a_recv, o_send, o_recv, l_send, l_recv,
    sib_send, sib_recv, x_send, x_recv, log_send, log_recv,
):
    seq = lax.axis_index("seq")
    head = lax.axis_index("head")
    n_seq = pair_in.shape[0]
    n_head = log_in.shape[0]
    rows = tok.shape[0]
    picked = pair_in.shape[1]
    hd = got_o.shape[3]
    heads = n_seq // 2
    core = lax.rem(head, 2)
    chip = head // 2
    sibling = head + 1 - 2 * core
    across = lax.rem(head + 2, n_head)

    barrier = pltpu.get_barrier_semaphore()
    for d in range(1, n_seq):
        pl.semaphore_signal(
            barrier, inc=1, device_id=(lax.rem(seq + d, n_seq), head), device_id_type=MESH
        )
    for d in range(1, n_head):
        pl.semaphore_signal(
            barrier, inc=1, device_id=(seq, lax.rem(head + d, n_head)), device_id_type=MESH
        )

    wide = wqkv.shape[2]
    halves = wqkv.shape[0] // 3
    ready = heads // halves
    loads = [
        pltpu.make_async_copy(tok_hbm, tok, load_sem.at[0]),
        pltpu.make_async_copy(wout_hbm, wout, load_sem.at[1]),
        pltpu.make_async_copy(gain_hbm, gain, load_sem.at[2]),
        pltpu.make_async_copy(wlabel_hbm, wlabel, load_sem.at[3]),
    ]

    def w_load(half, c):
        cols = pl.ds(pl.multiple_of(half * wide, wide), wide)
        k = half * 3 + c
        return pltpu.make_async_copy(wqkv_hbm.at[c, :, cols], wqkv.at[k], w_sem.at[k])

    loads[0].start()
    for half in range(halves):
        for c in range(3):
            w_load(half, c).start()

    def pair_copy(j):
        return pltpu.make_async_remote_copy(
            src_ref=pair_out.at[j], dst_ref=pair_in.at[seq],
            send_sem=a2a_send.at[j], recv_sem=a2a_recv.at[seq],
            device_id=(j, head), device_id_type=MESH,
        )

    def pair_arrival(i):
        return pltpu.make_async_remote_copy(
            src_ref=pair_out.at[i], dst_ref=pair_in.at[i],
            send_sem=a2a_send.at[i], recv_sem=a2a_recv.at[i],
            device_id=(i, head), device_id_type=MESH,
        )

    both = lax.broadcasted_iota(jnp.int32, (2 * picked, rows), 0)
    is_mid = both < picked
    sel_row = jnp.where(is_mid, both, both - picked) * SPAN
    sel_tok = lax.broadcasted_iota(jnp.int32, (2 * picked, rows), 1)
    loads[0].wait()

    def project_half(half):
        def project(c):
            w_load(half, c).wait()
            result = jnp.dot(
                tok[...], wqkv[half * 3 + c], preferred_element_type=jnp.float32
            ).astype(jnp.bfloat16)
            for i in range(ready):
                qkv[c, half * ready + i] = result[:, i * hd : (i + 1) * hd]

        repeat(0, 3, project)

        @pl.when(half == 0)
        def _():
            pl.semaphore_wait(barrier, n_seq + n_head - 2)

        for i in range(ready):
            h = half * ready + i
            mine = jnp.concatenate([qkv[c, h] for c in range(3)], axis=1)
            spot = sel_row + jnp.where(is_mid, off_mid[h], off_far[h])
            one_hot = (sel_tok == spot).astype(jnp.bfloat16)
            found = jnp.dot(one_hot, mine, preferred_element_type=jnp.float32).astype(
                jnp.bfloat16
            )
            for b in range(2):
                pair_out[b * heads + h] = found[b * picked : (b + 1) * picked]

        def send(d):
            turn = lax.rem(seq + d, 2 * ready)
            j = turn // ready * heads + half * ready + lax.rem(turn, ready)

            @pl.when(seq != j)
            def _():
                pair_copy(j).start()

        repeat(0, 2 * ready, send)

    repeat(0, halves, project_half)
    for load in loads[1:]:
        load.start()
    pair_in[seq] = pair_out[seq]

    chunks = x_in.shape[0]
    part = x_in.shape[1]
    width = x_in.shape[2]
    side = 2 * part
    def near_head(h):
        o, lse = softmax_parts(qkv[0, h], qkv[1, h], qkv[2, h])
        near_o[h] = o
        near_l[h] = lse

    repeat(0, heads, near_head)

    repeat(1, n_seq, lambda d: pair_arrival(lax.rem(seq + d, n_seq)).wait_recv())

    half_picked = picked // 2
    asked = n_seq * half_picked

    def o_copy(s, i, slot):
        return pltpu.make_async_remote_copy(
            src_ref=ret_o.at[s, i], dst_ref=got_o.at[s, slot],
            send_sem=o_send.at[s, i], recv_sem=o_recv.at[s, slot],
            device_id=(i, head), device_id_type=MESH,
        )

    def l_copy(s, i, slot):
        return pltpu.make_async_remote_copy(
            src_ref=ret_l.at[s], dst_ref=got_l.at[s, slot],
            send_sem=l_send.at[s, i], recv_sem=l_recv.at[s, slot],
            device_id=(i, head), device_id_type=MESH,
        )

    def answer(s):
        first = lax.rem(1 - chip + s, 2) * half_picked
        place = pl.ds(pl.multiple_of(first, half_picked), half_picked)
        pq = pair_in[:, place, 0:hd].reshape(asked, hd)
        pk, pv = (
            pair_in[:, :, c * hd : (c + 1) * hd].reshape(n_seq * picked, hd) for c in (1, 2)
        )
        o, lse = softmax_parts(pq, pk, pv)
        ret_o[s] = o.astype(jnp.bfloat16).reshape(n_seq, half_picked, hd)
        r0 = lax.broadcasted_iota(jnp.int32, (asked, asked), 0)
        r1 = lax.broadcasted_iota(jnp.int32, (asked, asked), 1)
        ret_l[s] = jnp.sum(jnp.where(r0 == r1, lse, 0.0), axis=0, keepdims=True)

        def send_back(d):
            i = lax.rem(seq + d, n_seq)
            o_copy(s, i, seq).start()
            l_copy(s, i, seq).start()

        repeat(1, n_seq, send_back)
        got_o[s, seq] = ret_o[s, seq]
        got_l[s, seq] = ret_l[s]

    repeat(0, 2, answer)
    base = seq * half_picked

    def merge(s, first, h):
        tok_col = lax.broadcasted_iota(jnp.int32, (side, hd), 0)
        lane = lax.broadcasted_iota(jnp.int32, (side, hd), 1) - base
        tok_sel = lax.broadcasted_iota(jnp.int32, (side, half_picked), 0)
        row_sel = lax.broadcasted_iota(jnp.int32, (side, half_picked), 1)
        tok_one = lax.broadcasted_iota(jnp.int32, (side, 1), 0)
        place = pl.ds(pl.multiple_of(first, side), side)
        terms = [(near_o[h, place, :], near_l[h, place, :])]
        marks = [None]
        for b, off in enumerate((off_mid, off_far)):
            j = b * heads + h
            spot = off[h]
            hit = lane * SPAN + spot == tok_col
            lse_col = jnp.sum(jnp.where(hit, got_l[s, j], 0.0), axis=-1, keepdims=True)
            one_hot = (tok_sel == row_sel * SPAN + spot).astype(jnp.bfloat16)
            spread = jnp.dot(one_hot, got_o[s, j], preferred_element_type=jnp.float32)
            mark = lax.rem(tok_one, SPAN) == spot
            terms.append((spread, jnp.where(mark, lse_col, -1e30)))
            marks.append(mark)
        peak = jnp.maximum(jnp.maximum(terms[0][1], terms[1][1]), terms[2][1])
        upper = jnp.zeros((side, hd), jnp.float32)
        lower = jnp.zeros((side, 1), jnp.float32)
        for (o, lse), mark in zip(terms, marks):
            factor = jnp.exp(lse - peak)
            if mark is not None:
                factor = jnp.where(mark, factor, 0.0)
            upper = upper + factor * o
            lower = lower + factor
        return (upper / lower).astype(jnp.bfloat16)

    def sib_copy(s, n):
        return pltpu.make_async_remote_copy(
            src_ref=parts.at[s, n, 1 - core], dst_ref=sib_in.at[s, n],
            send_sem=sib_send.at[s, n], recv_sem=sib_recv.at[s, n],
            device_id=(seq, sibling), device_id_type=MESH,
        )

    def x_copy(n):
        return pltpu.make_async_remote_copy(
            src_ref=x_out.at[n], dst_ref=x_in.at[n],
            send_sem=x_send.at[n], recv_sem=x_recv.at[n],
            device_id=(seq, across), device_id_type=MESH,
        )

    def pass_on(n):
        sib_copy(0, n).wait_recv()
        x_out[n] = (
            parts[0, n, core].astype(jnp.float32) + sib_in[0, n].astype(jnp.float32)
        ).astype(jnp.bfloat16)
        x_copy(n).start()

    for load in loads[1:]:
        load.wait()
    def project_side(s):
        first = lax.rem(1 - chip + s, 2) * side

        def returned(d):
            j = lax.rem(seq + d, n_seq)
            o_copy(s, j, j).wait_recv()
            l_copy(s, j, j).wait_recv()

        repeat(1, n_seq, returned)

        def merge_pair(g):
            for i in range(2):
                h = 2 * g + i
                attn[s, :, pl.ds(pl.multiple_of(h * hd, hd), hd)] = merge(s, first, h)

        repeat(0, heads // 2, merge_pair)

        def project_out(n):
            cols = pl.ds(pl.multiple_of(n * width, width), width)
            parts[s, n] = (
                jnp.dot(attn[s], wout[:, cols], preferred_element_type=jnp.float32)
                .astype(jnp.bfloat16)
                .reshape(2, part, width)
            )
            sib_copy(s, n).start()

            @pl.when((s == 0) & (n > 0))
            def _():
                pass_on(n - 1)

        repeat(0, chunks, project_out)

        @pl.when(s == 0)
        def _():
            pass_on(chunks - 1)

    repeat(0, 2, project_side)

    here = pl.ds(pl.multiple_of(head * part, part), part)

    def finish(n, carry):
        squares, product = carry
        cols = pl.ds(pl.multiple_of(n * width, width), width)
        sib_copy(1, n).wait_recv()
        x_copy(n).wait_recv()
        summed = parts[1, n, core].astype(jnp.float32) + sib_in[1, n].astype(jnp.float32)
        mixed = tok[here, cols].astype(jnp.float32) + (summed + x_in[n].astype(jnp.float32))
        squares = squares + jnp.sum(mixed * mixed, axis=-1, keepdims=True)
        scaled = (mixed * gain[:, cols]).astype(jnp.bfloat16)
        product = product + jnp.dot(scaled, wlabel[cols, :], preferred_element_type=jnp.float32)
        return squares, product

    squares, product = lax.fori_loop(
        0,
        chunks,
        finish,
        (jnp.zeros((part, 1), jnp.float32), jnp.zeros((part, wlabel.shape[1]), jnp.float32)),
    )
    log_out[...] = (product / jnp.sqrt(squares / tok.shape[1] + 1e-05)).astype(jnp.bfloat16)

    def log_copy(p, slot):
        return pltpu.make_async_remote_copy(
            src_ref=log_out, dst_ref=log_in.at[slot],
            send_sem=log_send.at[p], recv_sem=log_recv.at[slot],
            device_id=(seq, p), device_id_type=MESH,
        )

    for d in (2, 1, 3):
        log_copy(lax.rem(head + d, n_head), head).start()
    log_in[head] = log_out[...]
    for d in range(1, n_head):
        p = lax.rem(head + d, n_head)
        log_copy(p, p).wait_recv()
    for p in range(n_head):
        out_ref[p * part : (p + 1) * part, :] = log_in[p]

    def sent(d):
        j = lax.rem(seq + d, n_seq)
        pair_copy(j).wait_send()
        for s in range(2):
            o_copy(s, j, seq).wait_send()
            l_copy(s, j, seq).wait_send()

    repeat(1, n_seq, sent)

    def sent_parts(n):
        sib_copy(0, n).wait_send()
        sib_copy(1, n).wait_send()
        x_copy(n).wait_send()

    repeat(0, chunks, sent_parts)
    for d in range(1, n_head):
        log_copy(lax.rem(head + d, n_head), head).wait_send()


def fused_body(n_seq, n_head, tokens, w_qkv, w_out, norm_gain, w_label, offset_mid, offset_far):
    rows, width = tokens.shape
    heads = offset_mid.shape[0]
    own = w_qkv.shape[2]
    hd = own // heads
    classes = w_label.shape[1]
    picked = rows // SPAN
    part = rows // n_head
    chunks = 4
    span = width // chunks
    bf16, f32 = jnp.bfloat16, jnp.float32
    dma = pltpu.SemaphoreType.DMA
    anywhere = pl.BlockSpec(memory_space=pl.ANY)
    scalars = pl.BlockSpec(memory_space=pltpu.SMEM)
    return pl.pallas_call(
        kernel,
        out_shape=pltpu.VMEM((rows, classes), bf16),
        in_specs=[anywhere] * 5 + [scalars] * 2,
        out_specs=pl.BlockSpec(memory_space=pltpu.VMEM),
        scratch_shapes=[
            pltpu.VMEM((rows, width), bf16),
            pltpu.VMEM((6, width, own // 2), bf16),
            pltpu.VMEM((own, width), bf16),
            pltpu.VMEM((1, width), f32),
            pltpu.VMEM((width, classes), bf16),
            pltpu.VMEM((3, heads, rows, hd), bf16),
            pltpu.VMEM((heads, rows, hd), f32),
            pltpu.VMEM((heads, rows, 1), f32),
            pltpu.VMEM((n_seq, picked, 3 * hd), bf16),
            pltpu.VMEM((n_seq, picked, 3 * hd), bf16),
            pltpu.VMEM((2, n_seq, picked // 2, hd), bf16),
            pltpu.VMEM((2, 1, n_seq * picked // 2), f32),
            pltpu.VMEM((2, n_seq, picked // 2, hd), bf16),
            pltpu.VMEM((2, n_seq, 1, n_seq * picked // 2), f32),
            pltpu.VMEM((2, 2 * part, own), bf16),
            pltpu.VMEM((2, chunks, 2, part, span), bf16),
            pltpu.VMEM((2, chunks, part, span), bf16),
            pltpu.VMEM((chunks, part, span), bf16),
            pltpu.VMEM((chunks, part, span), bf16),
            pltpu.VMEM((part, classes), bf16),
            pltpu.VMEM((n_head, part, classes), bf16),
            dma((4,)), dma((6,)), dma((n_seq,)), dma((n_seq,)),
            dma((2, n_seq)), dma((2, n_seq)), dma((2, n_seq)), dma((2, n_seq)),
            dma((2, chunks)), dma((2, chunks)), dma((chunks,)), dma((chunks,)),
            dma((n_head,)), dma((n_head,)),
        ],
        compiler_params=pltpu.CompilerParams(
            collective_id=0, has_side_effects=True, vmem_limit_bytes=56 * 2**20
        ),
    )(
        tokens, jnp.transpose(w_qkv, (1, 0, 2)), w_out, norm_gain[None, :], w_label,
        offset_mid, offset_far,
    ).astype(f32)


def solution(mesh):
    n_seq, n_head = mesh.shape["seq"], mesh.shape["head"]
    run = body
    if n_seq == SPAN and n_head == 4:
        run = functools.partial(fused_body, n_seq, n_head)
    return jax.shard_map(
        run,
        mesh=mesh,
        in_specs=(
            P("seq", None),
            P(None, None, "head"),
            P("head", None),
            P(),
            P(),
            P("head"),
            P("head"),
        ),
        out_specs=P("seq", None),
        check_vma=False,
    )
```

```python
import functools

import jax
import jax.numpy as jnp
from jax import lax
from jax.experimental import pallas as pl
from jax.experimental.pallas import tpu as pltpu
from jax.sharding import PartitionSpec as P

MESH = pl.DeviceIdType.MESH

SPAN = 8


def from_behind(block, axis, distance):
    devices = range(lax.axis_size(axis))
    route = [((i - distance) % len(devices), i) for i in devices]
    return lax.ppermute(block, axis, route)


def attend(queries, keys, values):
    scores = jnp.einsum(
        "rhe,she->hrs", queries, keys, preferred_element_type=jnp.float32
    ) / jnp.sqrt(jnp.float32(queries.shape[2]))
    top = jnp.max(scores, axis=-1)
    weights = jnp.exp(scores - top[..., None])
    total = jnp.sum(weights, axis=-1)
    summed = jnp.einsum(
        "hrs,she->rhe", weights.astype(jnp.bfloat16), values, preferred_element_type=jnp.float32
    )
    return (top.T, total.T, summed)


def select_rows(array, offsets, rate):
    rows = array.shape[0] // rate
    shaped = array.reshape(rows, rate, array.shape[1], array.shape[2])
    marks = jnp.arange(rate, dtype=jnp.int32)[None, :, None] == offsets[None, None, :]
    return jnp.sum(jnp.where(marks[..., None], shaped, jnp.zeros_like(shaped)), axis=1)


def spread_rows(parts, offsets, rate):
    top, total, summed = parts
    rows = top.shape[0]
    marks = jnp.arange(rate, dtype=jnp.int32)[None, :, None] == offsets[None, None, :]
    top_full = jnp.where(marks, top[:, None, :], jnp.float32(-1e30)).reshape(rows * rate, -1)
    total_full = jnp.where(marks, total[:, None, :], jnp.float32(0.0)).reshape(rows * rate, -1)
    sum_full = jnp.where(marks[..., None], summed[:, None], jnp.float32(0.0)).reshape(
        rows * rate, summed.shape[1], summed.shape[2]
    )
    return (top_full, total_full, sum_full)


def body(tokens, w_qkv, w_out, norm_gain, w_label, offset_mid, offset_far):
    tok_rows = tokens.shape[0]
    local_heads = offset_mid.shape[0]
    head_size = w_qkv.shape[2] // local_heads
    qkv = jnp.einsum("td,dce->tce", tokens, w_qkv, preferred_element_type=jnp.float32).astype(
        jnp.bfloat16
    )
    qkv = qkv.reshape(tok_rows, 3, local_heads, head_size)
    queries, keys, values = (qkv[:, 0], qkv[:, 1], qkv[:, 2])
    seq_count = lax.axis_size("seq")
    near = attend(queries, keys, values)
    mid_q = select_rows(queries, offset_mid, SPAN)
    mid_kv = jnp.stack(
        [select_rows(keys, offset_mid, SPAN), select_rows(values, offset_mid, SPAN)], axis=0
    )
    mid_rows = mid_kv.shape[1]
    position = (lax.axis_index("seq") + SPAN // 2) % SPAN
    lower_pieces = []
    upper_pieces = []
    for step_back in range(1, SPAN):
        lower_pieces.insert(0, from_behind(mid_kv, "seq", step_back))
        upper_pieces.append(from_behind(mid_kv, "seq", -step_back))
    window = jnp.concatenate(lower_pieces + [mid_kv] + upper_pieces, axis=1)
    gathered = lax.dynamic_slice_in_dim(
        window, (SPAN - 1 - position) * mid_rows, SPAN * mid_rows, 1
    )
    middle = spread_rows(attend(mid_q, gathered[0], gathered[1]), offset_mid, SPAN)
    far_q = select_rows(queries, offset_far, seq_count)
    far_kv = jnp.stack(
        [select_rows(keys, offset_far, seq_count), select_rows(values, offset_far, seq_count)],
        axis=0,
    )
    far_all = lax.all_gather(far_kv, "seq", axis=1, tiled=True)
    distant = spread_rows(attend(far_q, far_all[0], far_all[1]), offset_far, seq_count)
    branches = [near, middle, distant]
    peak = jnp.maximum(jnp.maximum(near[0], middle[0]), distant[0])
    upper = jnp.zeros((tok_rows, local_heads, head_size), jnp.float32)
    lower = jnp.zeros((tok_rows, local_heads), jnp.float32)
    for top, total, summed in branches:
        factor = jnp.exp(top - peak)
        upper = upper + factor[..., None] * summed
        lower = lower + factor * total
    attn = (
        (upper / lower[..., None]).astype(jnp.bfloat16).reshape(tok_rows, local_heads * head_size)
    )
    partial_out = jnp.dot(attn, w_out, preferred_element_type=jnp.float32)
    projected = lax.psum(partial_out.astype(jnp.bfloat16), "head").astype(jnp.float32)
    mixed = tokens.astype(jnp.float32) + projected
    mean_sq = jnp.mean(mixed * mixed, axis=-1)
    scaled = (mixed * norm_gain).astype(jnp.bfloat16)
    product = jnp.dot(scaled, w_label, preferred_element_type=jnp.float32)
    return product / jnp.sqrt(mean_sq + 1e-05)[:, None]


def softmax_parts(queries, keys, values):
    scale = 1.0 / queries.shape[1] ** 0.5
    scores = (
        lax.dot_general(
            queries, keys, (((1,), (1,)), ((), ())), preferred_element_type=jnp.float32
        )
        * scale
    )
    top = jnp.max(scores, axis=-1, keepdims=True)
    weights = jnp.exp(scores - top)
    total = jnp.sum(weights, axis=-1, keepdims=True)
    summed = jnp.dot(weights.astype(jnp.bfloat16), values, preferred_element_type=jnp.float32)
    return summed / total, top + jnp.log(total)


def repeat(first, last, step):
    def run(i, carry):
        step(i)
        return carry

    lax.fori_loop(first, last, run, 0)


def kernel(
    tok_hbm, wqkv_hbm, wout_hbm, gain_hbm, wlabel_hbm, off_mid, off_far, out_ref,
    tok, wqkv, wout, gain, wlabel, qkv, near_o, near_l, pair_out, pair_in, ret_o, ret_l, got_o, got_l,
    attn, parts, sib_in, x_out, x_in, log_out, log_in,
    load_sem, w_sem, a2a_send, a2a_recv, o_send, o_recv, l_send, l_recv,
    sib_send, sib_recv, x_send, x_recv, log_send, log_recv,
):
    seq = lax.axis_index("seq")
    head = lax.axis_index("head")
    n_seq = pair_in.shape[0]
    n_head = log_in.shape[0]
    rows = tok.shape[0]
    picked = pair_in.shape[1]
    hd = got_o.shape[3]
    heads = n_seq // 2
    core = lax.rem(head, 2)
    chip = head // 2
    sibling = head + 1 - 2 * core
    across = lax.rem(head + 2, n_head)

    barrier = pltpu.get_barrier_semaphore()
    for d in range(1, n_seq):
        pl.semaphore_signal(
            barrier, inc=1, device_id=(lax.rem(seq + d, n_seq), head), device_id_type=MESH
        )
    for d in range(1, n_head):
        pl.semaphore_signal(
            barrier, inc=1, device_id=(seq, lax.rem(head + d, n_head)), device_id_type=MESH
        )

    wide = wqkv.shape[2]
    halves = wqkv.shape[0] // 3
    ready = heads // halves
    loads = [
        pltpu.make_async_copy(tok_hbm, tok, load_sem.at[0]),
        pltpu.make_async_copy(wout_hbm, wout, load_sem.at[1]),
        pltpu.make_async_copy(gain_hbm, gain, load_sem.at[2]),
        pltpu.make_async_copy(wlabel_hbm, wlabel, load_sem.at[3]),
    ]

    def w_load(half, c):
        cols = pl.ds(pl.multiple_of(half * wide, wide), wide)
        k = half * 3 + c
        return pltpu.make_async_copy(wqkv_hbm.at[c, :, cols], wqkv.at[k], w_sem.at[k])

    loads[0].start()
    for half in range(halves):
        for c in range(3):
            w_load(half, c).start()

    def pair_copy(j):
        return pltpu.make_async_remote_copy(
            src_ref=pair_out.at[j], dst_ref=pair_in.at[seq],
            send_sem=a2a_send.at[j], recv_sem=a2a_recv.at[seq],
            device_id=(j, head), device_id_type=MESH,
        )

    def pair_arrival(i):
        return pltpu.make_async_remote_copy(
            src_ref=pair_out.at[i], dst_ref=pair_in.at[i],
            send_sem=a2a_send.at[i], recv_sem=a2a_recv.at[i],
            device_id=(i, head), device_id_type=MESH,
        )

    both = lax.broadcasted_iota(jnp.int32, (2 * picked, rows), 0)
    is_mid = both < picked
    sel_row = jnp.where(is_mid, both, both - picked) * SPAN
    sel_tok = lax.broadcasted_iota(jnp.int32, (2 * picked, rows), 1)
    loads[0].wait()

    def project_half(half):
        def project(c):
            w_load(half, c).wait()
            result = jnp.dot(
                tok[...], wqkv[half * 3 + c], preferred_element_type=jnp.float32
            ).astype(jnp.bfloat16)
            for i in range(ready):
                qkv[c, half * ready + i] = result[:, i * hd : (i + 1) * hd]

        repeat(0, 3, project)

        @pl.when(half == 0)
        def _():
            pl.semaphore_wait(barrier, n_seq + n_head - 2)

        for i in range(ready):
            h = half * ready + i
            mine = jnp.concatenate([qkv[c, h] for c in range(3)], axis=1)
            spot = sel_row + jnp.where(is_mid, off_mid[h], off_far[h])
            one_hot = (sel_tok == spot).astype(jnp.bfloat16)
            found = jnp.dot(one_hot, mine, preferred_element_type=jnp.float32).astype(
                jnp.bfloat16
            )
            for b in range(2):
                pair_out[b * heads + h] = found[b * picked : (b + 1) * picked]

        def send(d):
            turn = lax.rem(seq + d, 2 * ready)
            j = turn // ready * heads + half * ready + lax.rem(turn, ready)

            @pl.when(seq != j)
            def _():
                pair_copy(j).start()

        repeat(0, 2 * ready, send)

    repeat(0, halves, project_half)
    for load in loads[1:]:
        load.start()
    pair_in[seq] = pair_out[seq]

    chunks = x_in.shape[0]
    part = x_in.shape[1]
    width = x_in.shape[2]
    side = 2 * part
    def near_head(h):
        o, lse = softmax_parts(qkv[0, h], qkv[1, h], qkv[2, h])
        near_o[h] = o
        near_l[h] = lse

    repeat(0, heads // 2, near_head)

    repeat(1, n_seq, lambda d: pair_arrival(lax.rem(seq + d, n_seq)).wait_recv())

    half_picked = picked // 2
    asked = n_seq * half_picked

    def o_copy(s, i, slot):
        return pltpu.make_async_remote_copy(
            src_ref=ret_o.at[s, i], dst_ref=got_o.at[s, slot],
            send_sem=o_send.at[s, i], recv_sem=o_recv.at[s, slot],
            device_id=(i, head), device_id_type=MESH,
        )

    def l_copy(s, i, slot):
        return pltpu.make_async_remote_copy(
            src_ref=ret_l.at[s], dst_ref=got_l.at[s, slot],
            send_sem=l_send.at[s, i], recv_sem=l_recv.at[s, slot],
            device_id=(i, head), device_id_type=MESH,
        )

    def answer(s):
        first = lax.rem(1 - chip + s, 2) * half_picked
        place = pl.ds(pl.multiple_of(first, half_picked), half_picked)
        pq = pair_in[:, place, 0:hd].reshape(asked, hd)
        pk, pv = (
            pair_in[:, :, c * hd : (c + 1) * hd].reshape(n_seq * picked, hd) for c in (1, 2)
        )
        o, lse = softmax_parts(pq, pk, pv)
        ret_o[s] = o.astype(jnp.bfloat16).reshape(n_seq, half_picked, hd)
        r0 = lax.broadcasted_iota(jnp.int32, (asked, asked), 0)
        r1 = lax.broadcasted_iota(jnp.int32, (asked, asked), 1)
        ret_l[s] = jnp.sum(jnp.where(r0 == r1, lse, 0.0), axis=0, keepdims=True)

        def send_back(d):
            i = lax.rem(seq + d, n_seq)
            o_copy(s, i, seq).start()
            l_copy(s, i, seq).start()

        repeat(1, n_seq, send_back)
        got_o[s, seq] = ret_o[s, seq]
        got_l[s, seq] = ret_l[s]

    repeat(0, 2, answer)
    repeat(heads // 2, heads, near_head)
    base = seq * half_picked

    def merge(s, first, h):
        tok_col = lax.broadcasted_iota(jnp.int32, (side, hd), 0)
        lane = lax.broadcasted_iota(jnp.int32, (side, hd), 1) - base
        tok_sel = lax.broadcasted_iota(jnp.int32, (side, half_picked), 0)
        row_sel = lax.broadcasted_iota(jnp.int32, (side, half_picked), 1)
        tok_one = lax.broadcasted_iota(jnp.int32, (side, 1), 0)
        place = pl.ds(pl.multiple_of(first, side), side)
        terms = [(near_o[h, place, :], near_l[h, place, :])]
        marks = [None]
        for b, off in enumerate((off_mid, off_far)):
            j = b * heads + h
            spot = off[h]
            hit = lane * SPAN + spot == tok_col
            lse_col = jnp.sum(jnp.where(hit, got_l[s, j], 0.0), axis=-1, keepdims=True)
            one_hot = (tok_sel == row_sel * SPAN + spot).astype(jnp.bfloat16)
            spread = jnp.dot(one_hot, got_o[s, j], preferred_element_type=jnp.float32)
            mark = lax.rem(tok_one, SPAN) == spot
            terms.append((spread, jnp.where(mark, lse_col, -1e30)))
            marks.append(mark)
        peak = jnp.maximum(jnp.maximum(terms[0][1], terms[1][1]), terms[2][1])
        upper = jnp.zeros((side, hd), jnp.float32)
        lower = jnp.zeros((side, 1), jnp.float32)
        for (o, lse), mark in zip(terms, marks):
            factor = jnp.exp(lse - peak)
            if mark is not None:
                factor = jnp.where(mark, factor, 0.0)
            upper = upper + factor * o
            lower = lower + factor
        return (upper / lower).astype(jnp.bfloat16)

    def sib_copy(s, n):
        return pltpu.make_async_remote_copy(
            src_ref=parts.at[s, n, 1 - core], dst_ref=sib_in.at[s, n],
            send_sem=sib_send.at[s, n], recv_sem=sib_recv.at[s, n],
            device_id=(seq, sibling), device_id_type=MESH,
        )

    def x_copy(n):
        return pltpu.make_async_remote_copy(
            src_ref=x_out.at[n], dst_ref=x_in.at[n],
            send_sem=x_send.at[n], recv_sem=x_recv.at[n],
            device_id=(seq, across), device_id_type=MESH,
        )

    def pass_on(n):
        sib_copy(0, n).wait_recv()
        x_out[n] = (
            parts[0, n, core].astype(jnp.float32) + sib_in[0, n].astype(jnp.float32)
        ).astype(jnp.bfloat16)
        x_copy(n).start()

    for load in loads[1:]:
        load.wait()
    def project_side(s):
        first = lax.rem(1 - chip + s, 2) * side

        def returned(d):
            j = lax.rem(seq + d, n_seq)
            o_copy(s, j, j).wait_recv()
            l_copy(s, j, j).wait_recv()

        repeat(1, n_seq, returned)

        def merge_pair(g):
            for i in range(2):
                h = 2 * g + i
                attn[s, :, pl.ds(pl.multiple_of(h * hd, hd), hd)] = merge(s, first, h)

        repeat(0, heads // 2, merge_pair)

        def project_out(n):
            cols = pl.ds(pl.multiple_of(n * width, width), width)
            parts[s, n] = (
                jnp.dot(attn[s], wout[:, cols], preferred_element_type=jnp.float32)
                .astype(jnp.bfloat16)
                .reshape(2, part, width)
            )
            sib_copy(s, n).start()

            @pl.when((s == 0) & (n > 0))
            def _():
                pass_on(n - 1)

        repeat(0, chunks, project_out)

        @pl.when(s == 0)
        def _():
            pass_on(chunks - 1)

    repeat(0, 2, project_side)

    here = pl.ds(pl.multiple_of(head * part, part), part)

    def finish(n, carry):
        squares, product = carry
        cols = pl.ds(pl.multiple_of(n * width, width), width)
        sib_copy(1, n).wait_recv()
        x_copy(n).wait_recv()
        summed = parts[1, n, core].astype(jnp.float32) + sib_in[1, n].astype(jnp.float32)
        mixed = tok[here, cols].astype(jnp.float32) + (summed + x_in[n].astype(jnp.float32))
        squares = squares + jnp.sum(mixed * mixed, axis=-1, keepdims=True)
        scaled = (mixed * gain[:, cols]).astype(jnp.bfloat16)
        product = product + jnp.dot(scaled, wlabel[cols, :], preferred_element_type=jnp.float32)
        return squares, product

    squares, product = lax.fori_loop(
        0,
        chunks,
        finish,
        (jnp.zeros((part, 1), jnp.float32), jnp.zeros((part, wlabel.shape[1]), jnp.float32)),
    )
    log_out[...] = (product / jnp.sqrt(squares / tok.shape[1] + 1e-05)).astype(jnp.bfloat16)

    def log_copy(p, slot):
        return pltpu.make_async_remote_copy(
            src_ref=log_out, dst_ref=log_in.at[slot],
            send_sem=log_send.at[p], recv_sem=log_recv.at[slot],
            device_id=(seq, p), device_id_type=MESH,
        )

    for d in (2, 1, 3):
        log_copy(lax.rem(head + d, n_head), head).start()
    log_in[head] = log_out[...]
    for d in range(1, n_head):
        p = lax.rem(head + d, n_head)
        log_copy(p, p).wait_recv()
    for p in range(n_head):
        out_ref[p * part : (p + 1) * part, :] = log_in[p]

    def sent(d):
        j = lax.rem(seq + d, n_seq)
        pair_copy(j).wait_send()
        for s in range(2):
            o_copy(s, j, seq).wait_send()
            l_copy(s, j, seq).wait_send()

    repeat(1, n_seq, sent)

    def sent_parts(n):
        sib_copy(0, n).wait_send()
        sib_copy(1, n).wait_send()
        x_copy(n).wait_send()

    repeat(0, chunks, sent_parts)
    for d in range(1, n_head):
        log_copy(lax.rem(head + d, n_head), head).wait_send()


def fused_body(n_seq, n_head, tokens, w_qkv, w_out, norm_gain, w_label, offset_mid, offset_far):
    rows, width = tokens.shape
    heads = offset_mid.shape[0]
    own = w_qkv.shape[2]
    hd = own // heads
    classes = w_label.shape[1]
    picked = rows // SPAN
    part = rows // n_head
    chunks = 4
    span = width // chunks
    bf16, f32 = jnp.bfloat16, jnp.float32
    dma = pltpu.SemaphoreType.DMA
    anywhere = pl.BlockSpec(memory_space=pl.ANY)
    scalars = pl.BlockSpec(memory_space=pltpu.SMEM)
    return pl.pallas_call(
        kernel,
        out_shape=pltpu.VMEM((rows, classes), bf16),
        in_specs=[anywhere] * 5 + [scalars] * 2,
        out_specs=pl.BlockSpec(memory_space=pltpu.VMEM),
        scratch_shapes=[
            pltpu.VMEM((rows, width), bf16),
            pltpu.VMEM((6, width, own // 2), bf16),
            pltpu.VMEM((own, width), bf16),
            pltpu.VMEM((1, width), f32),
            pltpu.VMEM((width, classes), bf16),
            pltpu.VMEM((3, heads, rows, hd), bf16),
            pltpu.VMEM((heads, rows, hd), f32),
            pltpu.VMEM((heads, rows, 1), f32),
            pltpu.VMEM((n_seq, picked, 3 * hd), bf16),
            pltpu.VMEM((n_seq, picked, 3 * hd), bf16),
            pltpu.VMEM((2, n_seq, picked // 2, hd), bf16),
            pltpu.VMEM((2, 1, n_seq * picked // 2), f32),
            pltpu.VMEM((2, n_seq, picked // 2, hd), bf16),
            pltpu.VMEM((2, n_seq, 1, n_seq * picked // 2), f32),
            pltpu.VMEM((2, 2 * part, own), bf16),
            pltpu.VMEM((2, chunks, 2, part, span), bf16),
            pltpu.VMEM((2, chunks, part, span), bf16),
            pltpu.VMEM((chunks, part, span), bf16),
            pltpu.VMEM((chunks, part, span), bf16),
            pltpu.VMEM((part, classes), bf16),
            pltpu.VMEM((n_head, part, classes), bf16),
            dma((4,)), dma((6,)), dma((n_seq,)), dma((n_seq,)),
            dma((2, n_seq)), dma((2, n_seq)), dma((2, n_seq)), dma((2, n_seq)),
            dma((2, chunks)), dma((2, chunks)), dma((chunks,)), dma((chunks,)),
            dma((n_head,)), dma((n_head,)),
        ],
        compiler_params=pltpu.CompilerParams(
            collective_id=0, has_side_effects=True, vmem_limit_bytes=56 * 2**20
        ),
    )(
        tokens, jnp.transpose(w_qkv, (1, 0, 2)), w_out, norm_gain[None, :], w_label,
        offset_mid, offset_far,
    ).astype(f32)


def solution(mesh):
    n_seq, n_head = mesh.shape["seq"], mesh.shape["head"]
    run = body
    if n_seq == SPAN and n_head == 4:
        run = functools.partial(fused_body, n_seq, n_head)
    return jax.shard_map(
        run,
        mesh=mesh,
        in_specs=(
            P("seq", None),
            P(None, None, "head"),
            P("head", None),
            P(),
            P(),
            P("head"),
            P("head"),
        ),
        out_specs=P("seq", None),
        check_vma=False,
    )
```
